32 devices in a mesh: groups: 2 (over y), seq: 16 (over z, x, core).
Axes of the slice: x: 2, y: 2, z: 4, core: 2. Of those that a mesh axis runs over, the one named last changes fastest.
Arguments:
- tokens: bfloat16 [8192, 256], P(('groups', 'seq')), parts along dimension 0, may hold values from -6 to 6
- norm_gain: float32 [256], replicated, may hold values from 0.1 to 1.9
- in_weight: bfloat16 [256, 768], replicated, may hold values from -0.375 to 0.375
- short_filter: float32 [3, 768], replicated, may hold values from -3 to 3
- spectra: bfloat16 [2, 256, 32, 256], P(None, None, 'seq'), may hold values from -6 to 6
- skip_gain: float32 [256], replicated, may hold values from -1 to 1
- out_weight: bfloat16 [256, 256], replicated, may hold values from -0.375 to 0.375
- mlp_gain: float32 [256], replicated, may hold values from 0.1 to 1.9
- up_weight: bfloat16 [256, 1024], replicated, may hold values from -0.375 to 0.375
- down_weight: bfloat16 [1024, 256], replicated, may hold values from -0.1875 to 0.1875
Outputs:
- result: bfloat16 [8192, 256], P(('groups', 'seq')), parts along dimension 0
The draws below stay inside these ranges and needn't reach their ends.
There are 2 independent parts, one for each index of `groups`. The reference program is written for one: setup_inputs(seed, part) draws one part's arguments, and reference() takes and returns one part's arrays. A program takes and returns all parts, laid end to end along the dimension named above; an argument that names none is the same for every part. Nothing has to cross between parts.
All inputs are finite; a program needn't handle non-finite values.
Results may differ from the reference program's by a relative error of at most 0.013.
Values may be sent and summed in bfloat16 or wider, within the bound.
A program may use at most 64 MiB of HBM per device.

```python
import jax
import jax.numpy as jnp
from jax import lax

D = 256
FF = 1024
KS = 3
LENGTH = 4096
NFFT = 8192
N2 = 256
N1 = 32


def level_of(stream_key, extent, split, low, largest):
    loudness = 1.0
    for dim, blocks in split:
        steps = jax.random.uniform(jax.random.fold_in(jax.random.fold_in(stream_key, 6), dim), (blocks,), jnp.float32, low / len(split), largest / len(split))
        loudness = loudness * jnp.repeat(jnp.exp(steps), extent[dim] // blocks).reshape((-1,) + (1,) * (len(extent) - 1 - dim))
    return loudness


def gaussian(own_key, shape, width, limit, split=(), kind=jnp.bfloat16):
    drawn = width * jax.random.normal(own_key, shape, jnp.float32)
    if split:
        drawn = drawn * level_of(own_key, shape, split, -0.22, 0.18)
    return jnp.clip(drawn, -limit, limit).astype(kind)


def setup_inputs(seed: int = 0, part: int = 0) -> dict:
    arg_keys = jax.random.split(jax.random.key(seed), 11)
    own_keys = jax.random.split(jax.random.fold_in(arg_keys[10], part), 11)
    tokens = gaussian(own_keys[0], (LENGTH, D), 1.0, 6.0, ((0, 16),))
    norm_gain = jnp.clip(1.0 + 0.18 * jax.random.normal(arg_keys[1], (D,), jnp.float32), 0.1, 1.9)
    in_weight = gaussian(arg_keys[2], (D, 3 * D), D ** -0.5, 0.375)
    short_filter = gaussian(arg_keys[3], (KS, 3 * D), 0.6, 3.0, (), jnp.float32)
    spectra = gaussian(arg_keys[4], (2, D, N1, N2), 1.0, 6.0, ((2, 16),))
    skip_gain = jnp.clip(jax.random.uniform(arg_keys[5], (D,), jnp.float32, -1.0, 1.0), -1.0, 1.0)
    out_weight = gaussian(arg_keys[6], (D, D), D ** -0.5, 0.375)
    mlp_gain = jnp.clip(1.0 + 0.18 * jax.random.normal(arg_keys[7], (D,), jnp.float32), 0.1, 1.9)
    up_weight = gaussian(arg_keys[8], (D, FF), D ** -0.5, 0.375)
    down_weight = gaussian(arg_keys[9], (FF, D), FF ** -0.5, 0.1875)
    return {"tokens": tokens, "norm_gain": norm_gain, "in_weight": in_weight, "short_filter": short_filter, "spectra": spectra, "skip_gain": skip_gain, "out_weight": out_weight, "mlp_gain": mlp_gain, "up_weight": up_weight, "down_weight": down_weight}


def rms_scale(values, gain):
    wide = values.astype(jnp.float32)
    return wide * lax.rsqrt(lax.optimization_barrier(jnp.mean(wide * wide, axis=-1, keepdims=True)) + 1e-06) * gain

def reference(tokens, norm_gain, in_weight, short_filter, spectra, skip_gain, out_weight, mlp_gain, up_weight, down_weight):
    normed = rms_scale(tokens, norm_gain).astype(jnp.bfloat16)
    projected = jnp.dot(normed, in_weight, preferred_element_type=jnp.float32).astype(jnp.bfloat16)
    padded = jnp.pad(projected.astype(jnp.float32), ((KS - 1, 0), (0, 0)))
    mixed = short_filter[0] * padded[KS - 1:]
    for lag in range(1, KS):
        mixed = mixed + short_filter[lag] * padded[KS - 1 - lag:KS - 1 - lag + LENGTH]
    query = mixed[:, :D].astype(jnp.bfloat16)
    driven = (mixed[:, D:2 * D] * mixed[:, 2 * D:]).astype(jnp.bfloat16)
    block = 16
    signal = driven.astype(jnp.float32).T.reshape(D // block, block, LENGTH)
    filt_real = spectra[0].astype(jnp.float32).transpose(0, 2, 1).reshape(D // block, block, NFFT)
    filt_imag = spectra[1].astype(jnp.float32).transpose(0, 2, 1).reshape(D // block, block, NFFT)

    def convolve(pieces):
        span_signal, span_real, span_imag = pieces
        extended = jnp.pad(span_signal, ((0, 0), (0, NFFT - LENGTH)))
        freq = jnp.fft.fft(extended, axis=1)
        back = jnp.fft.ifft(freq * lax.complex(span_real, span_imag), axis=1)
        return jnp.real(back)[:, :LENGTH]
    conv = lax.map(convolve, (signal, filt_real, filt_imag)).reshape(D, LENGTH).T
    response = conv + skip_gain * driven.astype(jnp.float32)
    gated = (query.astype(jnp.float32) * response).astype(jnp.bfloat16)
    hidden_state = (tokens.astype(jnp.float32) + jnp.dot(gated, out_weight, preferred_element_type=jnp.float32)).astype(jnp.bfloat16)
    second_norm = rms_scale(hidden_state, mlp_gain).astype(jnp.bfloat16)
    activated = jax.nn.gelu(jnp.dot(second_norm, up_weight, preferred_element_type=jnp.float32), approximate=True).astype(jnp.bfloat16)
    return (hidden_state.astype(jnp.float32) + jnp.dot(activated, down_weight, preferred_element_type=jnp.float32)).astype(jnp.bfloat16)
```

```python
import functools
import math

import jax
import jax.numpy as jnp
import ml_dtypes
import numpy as np
from jax import lax
from jax.experimental import pallas as pl
from jax.experimental.pallas import tpu as pltpu
from jax.sharding import PartitionSpec as P

exact = lax.Precision.HIGHEST
epsilon = 1e-06


def passed_along(value, axis, steps):
    count = lax.axis_size(axis)
    first, last = (max(0, -steps), min(count, count - steps))
    return lax.ppermute(value, axis, [(source, source + steps) for source in range(first, last)])


def as_sent(array):
    return jax.tree.map(lambda a: a.astype(jnp.bfloat16) if a.dtype == jnp.float32 else a, array)


def rms_scale(values, gain):
    wide = values.astype(jnp.float32)
    return wide * lax.rsqrt(jnp.mean(wide * wide, axis=-1, keepdims=True) + epsilon) * gain


def phase_table(out_start, out_count, in_start, in_count, period):
    index_out = out_start + lax.iota(jnp.int32, out_count)[:, None]
    index_in = in_start + lax.iota(jnp.int32, in_count)[None, :]
    angle = 2.0 * math.pi / period * (index_out * index_in % period).astype(jnp.float32)
    return (jnp.cos(angle), jnp.sin(angle))


def apply_filter(spec_real, spec_imag, filt):
    filt_real = filt[0].astype(jnp.float32)
    filt_imag = filt[1].astype(jnp.float32)
    return (
        spec_real * filt_real - spec_imag * filt_imag,
        spec_real * filt_imag + spec_imag * filt_real,
    )


def rows_forward_first(piece, column_start, total):
    half = piece.shape[0]
    length = 2 * half
    count = piece.shape[1]
    cosine, sine = phase_table(0, length, 0, half, length)
    wide = piece.astype(jnp.float32)
    real_part = jnp.einsum("kn,nmc->kmc", cosine, wide, precision=exact)
    imag_part = -jnp.einsum("kn,nmc->kmc", sine, wide, precision=exact)
    turn_cos, turn_sin = phase_table(0, length, column_start, count, total)
    turn_cos = turn_cos[:, :, None]
    turn_sin = turn_sin[:, :, None]
    return (
        real_part * turn_cos + imag_part * turn_sin,
        imag_part * turn_cos - real_part * turn_sin,
    )


def rows_forward_second(parts):
    real_part, imag_part = parts
    size = real_part.shape[1]
    cosine, sine = phase_table(0, size, 0, size, size)
    real_cos = jnp.einsum("kn,anc->akc", cosine, real_part, precision=exact)
    real_sin = jnp.einsum("kn,anc->akc", sine, real_part, precision=exact)
    imag_cos = jnp.einsum("kn,anc->akc", cosine, imag_part, precision=exact)
    imag_sin = jnp.einsum("kn,anc->akc", sine, imag_part, precision=exact)
    return (real_cos + imag_sin, imag_cos - real_sin)


def rows_inverse_second(real_part, imag_part, row_start, total):
    rows = real_part.shape[0]
    size = real_part.shape[1]
    cosine, sine = phase_table(0, size, 0, size, size)
    real_cos = jnp.einsum("nk,akc->anc", cosine, real_part, precision=exact)
    real_sin = jnp.einsum("nk,akc->anc", sine, real_part, precision=exact)
    imag_cos = jnp.einsum("nk,akc->anc", cosine, imag_part, precision=exact)
    imag_sin = jnp.einsum("nk,akc->anc", sine, imag_part, precision=exact)
    out_real = real_cos - imag_sin
    out_imag = real_sin + imag_cos
    turn_cos, turn_sin = phase_table(row_start, rows, 0, size, total)
    turn_cos = turn_cos[:, :, None]
    turn_sin = turn_sin[:, :, None]
    return (out_real * turn_cos - out_imag * turn_sin, out_real * turn_sin + out_imag * turn_cos)


def rows_inverse_first(parts, total):
    real_part, imag_part = parts
    length = real_part.shape[0]
    half = length // 2
    cosine, sine = phase_table(0, half, 0, length, length)
    summed = jnp.einsum("nk,kmc->nmc", cosine, real_part, precision=exact) - jnp.einsum(
        "nk,kmc->nmc", sine, imag_part, precision=exact
    )
    return summed / total


def local(
    tokens,
    norm_gain,
    in_weight,
    short_filter,
    spectra,
    skip_gain,
    out_weight,
    mlp_gain,
    up_weight,
    down_weight,
):
    tok_rows, width = tokens.shape
    devices = lax.axis_size("seq")
    position = lax.axis_index("seq")
    total = 2 * tok_rows * devices
    inner = min(tok_rows, 512)
    outer = total // inner
    normed = rms_scale(tokens, norm_gain).astype(jnp.bfloat16)
    projected = jnp.dot(normed, in_weight, preferred_element_type=jnp.float32).astype(jnp.bfloat16)
    taps = short_filter.shape[0]
    earlier = passed_along(projected[tok_rows - (taps - 1) :], "seq", 1)
    extended = jnp.concatenate([earlier, projected], axis=0).astype(jnp.float32)
    mixed = short_filter[0] * extended[taps - 1 :]
    for lag in range(1, taps):
        mixed = mixed + short_filter[lag] * extended[taps - 1 - lag : taps - 1 - lag + tok_rows]
    query = mixed[:, :width].astype(jnp.bfloat16)
    driven = (mixed[:, width : 2 * width] * mixed[:, 2 * width :]).astype(jnp.bfloat16)
    local_cols = inner // devices
    col_start = position * local_cols
    blocked = driven.reshape(tok_rows // inner, inner, width)
    piece = lax.all_to_all(blocked, "seq", split_axis=1, concat_axis=0, tiled=True)
    real_part, imag_part = rows_forward_first(piece, col_start, total)
    spec_real, spec_imag = rows_forward_second(
        (
            lax.all_to_all(
                real_part.astype(jnp.bfloat16), "seq", split_axis=0, concat_axis=1, tiled=True
            ).astype(real_part.dtype),
            lax.all_to_all(
                imag_part.astype(jnp.bfloat16), "seq", split_axis=0, concat_axis=1, tiled=True
            ).astype(imag_part.dtype),
        )
    )
    resident = jnp.transpose(spectra, (0, 2, 3, 1))
    prod_real, prod_imag = apply_filter(spec_real, spec_imag, resident)
    local_rows = outer // devices
    back_real, back_imag = rows_inverse_second(prod_real, prod_imag, position * local_rows, total)
    response_cols = rows_inverse_first(
        (
            lax.all_to_all(
                as_sent(back_real), "seq", split_axis=1, concat_axis=0, tiled=True
            ).astype(back_real.dtype),
            lax.all_to_all(
                as_sent(back_imag), "seq", split_axis=1, concat_axis=0, tiled=True
            ).astype(back_imag.dtype),
        ),
        total,
    )
    response_cols = response_cols + skip_gain[None, None, :] * piece.astype(jnp.float32)
    response = lax.all_to_all(
        response_cols, "seq", split_axis=0, concat_axis=1, tiled=True
    ).reshape(tok_rows, width)
    gated = (query.astype(jnp.float32) * response).astype(jnp.bfloat16)
    hidden_state = (
        tokens.astype(jnp.float32) + jnp.dot(gated, out_weight, preferred_element_type=jnp.float32)
    ).astype(jnp.bfloat16)
    second_norm = rms_scale(hidden_state, mlp_gain).astype(jnp.bfloat16)
    activated = jax.nn.gelu(
        jnp.dot(second_norm, up_weight, preferred_element_type=jnp.float32), approximate=True
    ).astype(jnp.bfloat16)
    return (
        hidden_state.astype(jnp.float32)
        + jnp.dot(activated, down_weight, preferred_element_type=jnp.float32)
    ).astype(jnp.bfloat16)


MESH = pl.DeviceIdType.MESH


def dft_tables(n, outer, inner, groups, share):
    kl = outer // n
    k1 = np.arange(outer)
    ang = 2.0 * np.pi * (np.outer(k1, np.arange(n)) % outer) / outer
    weights = np.stack([np.cos(ang), -np.sin(ang)]).reshape(2, n, kl, n)
    first = np.einsum("rpkn,gh,ij->rgpiknhj", weights, np.eye(groups), np.eye(share))
    first = first.reshape(2 * groups * outer * share, n * groups * share)
    ang = 2.0 * np.pi * (np.outer(np.arange(inner), np.arange(inner)) % inner) / inner
    cos, sin = np.cos(ang), np.sin(ang)
    second = np.block([[cos, -sin], [sin, cos]])
    ang = 2.0 * np.pi * np.outer(k1, np.arange(inner)) / (outer * inner)
    turn = np.stack([np.cos(ang), np.sin(ang)]).reshape(2, n, 1, kl, inner)
    turn = np.broadcast_to(turn, (2, n, share, kl, inner)).reshape(2, n * share * kl, inner)
    low = lambda a: a.astype(ml_dtypes.bfloat16)
    return low(first), low(np.ascontiguousarray(first.T)), low(second), turn.astype(np.float32)


def kernel(
    groups, n, share,
    tokens, norm_gain, in_weight, short_filter, skip_gain, mlp_gain,
    spectra, out_hbm, up_hbm, down_hbm, first_hbm, last_hbm, second_hbm, turn_hbm,
    result,
    filt, halo, extended, sent, signal, back, response,
    out_weight, up_weight, down_weight, first, last, second, turn,
    local_sem, filt_send, filt_recv, halo_send, halo_recv,
    sig_send, sig_recv, resp_send, resp_recv,
):
    count = groups * n
    group = lax.axis_index("groups")
    position = lax.axis_index("seq")
    me = position * groups + group
    rows, width = tokens.shape
    taps = short_filter.shape[0]

    def place(index):
        return (lax.rem(index, groups), lax.div(index, groups))

    barrier = pltpu.get_barrier_semaphore()

    def greet(step, carry):
        pl.semaphore_signal(
            barrier, inc=1, device_id=place(lax.rem(me + step, count)), device_id_type=MESH
        )
        return carry

    lax.fori_loop(1, count, greet, 0)

    pairs = (
        (first_hbm, first), (second_hbm, second), (turn_hbm, turn), (last_hbm, last),
        (out_hbm, out_weight), (up_hbm, up_weight), (down_hbm, down_weight),
    )
    loads = [
        pltpu.make_async_copy(source, target, local_sem.at[i])
        for i, (source, target) in enumerate(pairs)
    ]

    def channels(seq_index):
        return pl.ds((seq_index * groups + group) * share, share)

    own_filter = pltpu.make_async_copy(
        spectra.at[:, channels(position)], filt.at[position], local_sem.at[len(pairs)]
    )

    def filter_copy(target, source):
        return pltpu.make_async_remote_copy(
            src_ref=spectra.at[:, channels(target)], dst_ref=filt.at[source],
            send_sem=filt_send.at[target], recv_sem=filt_recv.at[source],
            device_id=(group, target), device_id_type=MESH,
        )

    def halo_copy(target):
        return pltpu.make_async_remote_copy(
            src_ref=tokens.at[pl.ds(rows - 16, 16)], dst_ref=halo,
            send_sem=halo_send.at[0], recv_sem=halo_recv.at[0],
            device_id=(group, target), device_id_type=MESH,
        )

    def signal_copy(target, source):
        return pltpu.make_async_remote_copy(
            src_ref=sent.at[target], dst_ref=signal.at[source],
            send_sem=sig_send.at[target], recv_sem=sig_recv.at[source],
            device_id=place(target), device_id_type=MESH,
        )

    def response_copy(target, source):
        return pltpu.make_async_remote_copy(
            src_ref=back.at[target], dst_ref=response.at[source],
            send_sem=resp_send.at[target], recv_sem=resp_recv.at[source],
            device_id=place(target), device_id_type=MESH,
        )

    def each(total, own, action):
        def body(step, carry):
            action(lax.rem(own + step, total))
            return carry

        lax.fori_loop(1, total, body, 0)

    for load in loads:
        load.start()
    own_filter.start()
    pl.semaphore_wait(barrier, count - 1)

    @pl.when(position < n - 1)
    def _():
        halo_copy(position + 1).start()

    @pl.when(position == 0)
    def _():
        halo[...] = jnp.zeros_like(halo)

    each(n, position, lambda other: filter_copy(other, position).start())

    gain = norm_gain[...].reshape(1, width)
    weight = in_weight[...]

    def project(values):
        normed = rms_scale(values, gain).astype(jnp.bfloat16)
        made = jnp.dot(normed, weight, preferred_element_type=jnp.float32)
        return made.astype(jnp.bfloat16).astype(jnp.float32)

    extended[pl.ds(8, rows), :] = project(tokens[...])

    @pl.when(position > 0)
    def _():
        halo_copy(position).wait_recv()

    extended[pl.ds(0, 8), :] = project(halo[...])[8:, :]
    mixed = short_filter[0:1, :] * extended[pl.ds(8, rows), :]
    for lag in range(1, taps):
        mixed = mixed + short_filter[lag : lag + 1, :] * extended[pl.ds(8 - lag, rows), :]
    query = mixed[:, :width].astype(jnp.bfloat16).astype(jnp.float32)
    driven = (mixed[:, width : 2 * width] * mixed[:, 2 * width :]).astype(jnp.bfloat16)
    driven = driven.astype(jnp.float32)
    sent[...] = driven.T.reshape(count, share, rows).astype(jnp.bfloat16)
    each(count, me, lambda other: signal_copy(other, me).start())
    signal[pl.ds(me, 1)] = sent[pl.ds(me, 1)]

    for load in loads:
        load.wait()
    own_filter.wait()
    each(count, me, lambda other: signal_copy(me, other).wait_recv())

    half = groups * n * share * (filt.shape[3])
    bins = half // groups
    gathered = signal[...].astype(jnp.float32).reshape(count * share, rows).astype(jnp.bfloat16)
    part = jnp.dot(first[...], gathered, preferred_element_type=jnp.float32)
    part_real = part[:half].reshape(groups, bins, rows)
    part_imag = part[half:].reshape(groups, bins, rows)
    turn_cos, turn_sin = turn[0][None], turn[1][None]
    turned = jnp.concatenate(
        [part_real * turn_cos + part_imag * turn_sin, part_imag * turn_cos - part_real * turn_sin],
        axis=-1,
    ).reshape(half, 2 * rows).astype(jnp.bfloat16)
    spec = jnp.dot(turned, second[...], preferred_element_type=jnp.float32)
    spec_real = spec[:, :rows].reshape(groups, bins, rows)
    spec_imag = spec[:, rows:].reshape(groups, bins, rows)
    each(n, position, lambda other: filter_copy(position, other).wait_recv())
    filt_real = filt[:, 0].astype(jnp.float32).reshape(1, bins, rows)
    filt_imag = filt[:, 1].astype(jnp.float32).reshape(1, bins, rows)
    product = jnp.concatenate(
        [
            spec_real * filt_real - spec_imag * filt_imag,
            -(spec_real * filt_imag + spec_imag * filt_real),
        ],
        axis=-1,
    ).reshape(half, 2 * rows).astype(jnp.bfloat16)
    inner_back = jnp.dot(product, second[...], preferred_element_type=jnp.float32)
    back_real = inner_back[:, :rows].reshape(groups, bins, rows)
    back_imag = inner_back[:, rows:].reshape(groups, bins, rows)
    turned_back = jnp.concatenate(
        [
            (back_real * turn_cos + back_imag * turn_sin).reshape(half, rows),
            (back_real * turn_sin - back_imag * turn_cos).reshape(half, rows),
        ],
        axis=0,
    ).astype(jnp.bfloat16)
    total = 2 * n * rows
    conv = jnp.dot(last[...], turned_back, preferred_element_type=jnp.float32) * (1.0 / total)
    back[...] = conv.reshape(count, share, rows).astype(jnp.bfloat16)
    each(count, me, lambda other: response_copy(other, me).start())
    response[pl.ds(me, 1)] = back[pl.ds(me, 1)]
    each(count, me, lambda other: response_copy(me, other).wait_recv())

    answer = response[...].astype(jnp.float32).reshape(width, rows).T
    answer = answer + skip_gain[...].reshape(1, width) * driven
    gated = (query * answer).astype(jnp.bfloat16)
    hidden = (
        tokens[...].astype(jnp.float32)
        + jnp.dot(gated, out_weight[...], preferred_element_type=jnp.float32)
    ).astype(jnp.bfloat16)
    second_norm = rms_scale(hidden, mlp_gain[...].reshape(1, width)).astype(jnp.bfloat16)
    activated = jax.nn.gelu(
        jnp.dot(second_norm, up_weight[...], preferred_element_type=jnp.float32), approximate=True
    ).astype(jnp.bfloat16)
    result[...] = (
        hidden.astype(jnp.float32)
        + jnp.dot(activated, down_weight[...], preferred_element_type=jnp.float32)
    ).astype(jnp.bfloat16)

    @pl.when(position < n - 1)
    def _():
        halo_copy(position + 1).wait_send()

    each(n, position, lambda other: filter_copy(other, position).wait_send())
    each(count, me, lambda other: signal_copy(other, me).wait_send())
    each(count, me, lambda other: response_copy(other, me).wait_send())


def fused(
    tokens, norm_gain, in_weight, short_filter, spectra, skip_gain,
    out_weight, mlp_gain, up_weight, down_weight,
):
    rows, width = tokens.shape
    groups, n = lax.axis_size("groups"), lax.axis_size("seq")
    count = groups * n
    share = width // count
    local_outer = spectra.shape[2]
    first, last, second, turn = dft_tables(n, n * local_outer, rows, groups, share)
    low = jnp.bfloat16
    vmem = pl.BlockSpec(memory_space=pltpu.VMEM)
    far = pl.BlockSpec(memory_space=pl.ANY)
    dma = pltpu.SemaphoreType.DMA
    held = [out_weight, up_weight, down_weight, first, last, second, turn]
    return pl.pallas_call(
        functools.partial(kernel, groups, n, share),
        out_shape=jax.ShapeDtypeStruct((rows, width), low),
        in_specs=[vmem] * 6 + [far] * 8,
        out_specs=vmem,
        scratch_shapes=[
            pltpu.VMEM((n, 2, share, local_outer, rows), low),
            pltpu.VMEM((16, width), low),
            pltpu.VMEM((rows + 8, 3 * width), jnp.float32),
            pltpu.VMEM((count, share, rows), low),
            pltpu.VMEM((count, share, rows), low),
            pltpu.VMEM((count, share, rows), low),
            pltpu.VMEM((count, share, rows), low),
        ]
        + [pltpu.VMEM(a.shape, a.dtype) for a in held]
        + [
            dma((8,)), dma((n,)), dma((n,)), dma((1,)), dma((1,)),
            dma((count,)), dma((count,)), dma((count,)), dma((count,)),
        ],
        compiler_params=pltpu.CompilerParams(
            collective_id=0, has_side_effects=True, vmem_limit_bytes=40 * 1024 * 1024
        ),
    )(
        tokens, norm_gain, in_weight, short_filter, skip_gain, mlp_gain,
        spectra, out_weight, up_weight, down_weight, first, last, second, turn,
    )


def solution(mesh):
    in_specs = (
        P(("groups", "seq"), None),
        P(),
        P(),
        P(),
        P(None, None, "seq", None),
        P(),
        P(),
        P(),
        P(),
        P(),
    )
    out_specs = P(("groups", "seq"), None)

    def layer(*args):
        rows, width = args[0].shape
        spectra = args[4]
        fits = (
            width % (8 * mesh.size) == 0
            and rows == spectra.shape[3]
            and spectra.shape[2] == 2
            and rows % 128 == 0
        )
        return (fused if fits else local)(*args)

    return jax.shard_map(layer, mesh=mesh, in_specs=in_specs, out_specs=out_specs, check_vma=False)
```

```python
import functools
import math

import jax
import jax.numpy as jnp
import ml_dtypes
import numpy as np
from jax import lax
from jax.experimental import pallas as pl
from jax.experimental.pallas import tpu as pltpu
from jax.sharding import PartitionSpec as P

exact = lax.Precision.HIGHEST
epsilon = 1e-06


def passed_along(value, axis, steps):
    count = lax.axis_size(axis)
    first, last = (max(0, -steps), min(count, count - steps))
    return lax.ppermute(value, axis, [(source, source + steps) for source in range(first, last)])


def as_sent(array):
    return jax.tree.map(lambda a: a.astype(jnp.bfloat16) if a.dtype == jnp.float32 else a, array)


def rms_scale(values, gain):
    wide = values.astype(jnp.float32)
    return wide * lax.rsqrt(jnp.mean(wide * wide, axis=-1, keepdims=True) + epsilon) * gain


def phase_table(out_start, out_count, in_start, in_count, period):
    index_out = out_start + lax.iota(jnp.int32, out_count)[:, None]
    index_in = in_start + lax.iota(jnp.int32, in_count)[None, :]
    angle = 2.0 * math.pi / period * (index_out * index_in % period).astype(jnp.float32)
    return (jnp.cos(angle), jnp.sin(angle))


def apply_filter(spec_real, spec_imag, filt):
    filt_real = filt[0].astype(jnp.float32)
    filt_imag = filt[1].astype(jnp.float32)
    return (
        spec_real * filt_real - spec_imag * filt_imag,
        spec_real * filt_imag + spec_imag * filt_real,
    )


def rows_forward_first(piece, column_start, total):
    half = piece.shape[0]
    length = 2 * half
    count = piece.shape[1]
    cosine, sine = phase_table(0, length, 0, half, length)
    wide = piece.astype(jnp.float32)
    real_part = jnp.einsum("kn,nmc->kmc", cosine, wide, precision=exact)
    imag_part = -jnp.einsum("kn,nmc->kmc", sine, wide, precision=exact)
    turn_cos, turn_sin = phase_table(0, length, column_start, count, total)
    turn_cos = turn_cos[:, :, None]
    turn_sin = turn_sin[:, :, None]
    return (
        real_part * turn_cos + imag_part * turn_sin,
        imag_part * turn_cos - real_part * turn_sin,
    )


def rows_forward_second(parts):
    real_part, imag_part = parts
    size = real_part.shape[1]
    cosine, sine = phase_table(0, size, 0, size, size)
    real_cos = jnp.einsum("kn,anc->akc", cosine, real_part, precision=exact)
    real_sin = jnp.einsum("kn,anc->akc", sine, real_part, precision=exact)
    imag_cos = jnp.einsum("kn,anc->akc", cosine, imag_part, precision=exact)
    imag_sin = jnp.einsum("kn,anc->akc", sine, imag_part, precision=exact)
    return (real_cos + imag_sin, imag_cos - real_sin)


def rows_inverse_second(real_part, imag_part, row_start, total):
    rows = real_part.shape[0]
    size = real_part.shape[1]
    cosine, sine = phase_table(0, size, 0, size, size)
    real_cos = jnp.einsum("nk,akc->anc", cosine, real_part, precision=exact)
    real_sin = jnp.einsum("nk,akc->anc", sine, real_part, precision=exact)
    imag_cos = jnp.einsum("nk,akc->anc", cosine, imag_part, precision=exact)
    imag_sin = jnp.einsum("nk,akc->anc", sine, imag_part, precision=exact)
    out_real = real_cos - imag_sin
    out_imag = real_sin + imag_cos
    turn_cos, turn_sin = phase_table(row_start, rows, 0, size, total)
    turn_cos = turn_cos[:, :, None]
    turn_sin = turn_sin[:, :, None]
    return (out_real * turn_cos - out_imag * turn_sin, out_real * turn_sin + out_imag * turn_cos)


def rows_inverse_first(parts, total):
    real_part, imag_part = parts
    length = real_part.shape[0]
    half = length // 2
    cosine, sine = phase_table(0, half, 0, length, length)
    summed = jnp.einsum("nk,kmc->nmc", cosine, real_part, precision=exact) - jnp.einsum(
        "nk,kmc->nmc", sine, imag_part, precision=exact
    )
    return summed / total


def local(
    tokens,
    norm_gain,
    in_weight,
    short_filter,
    spectra,
    skip_gain,
    out_weight,
    mlp_gain,
    up_weight,
    down_weight,
):
    tok_rows, width = tokens.shape
    devices = lax.axis_size("seq")
    position = lax.axis_index("seq")
    total = 2 * tok_rows * devices
    inner = min(tok_rows, 512)
    outer = total // inner
    normed = rms_scale(tokens, norm_gain).astype(jnp.bfloat16)
    projected = jnp.dot(normed, in_weight, preferred_element_type=jnp.float32).astype(jnp.bfloat16)
    taps = short_filter.shape[0]
    earlier = passed_along(projected[tok_rows - (taps - 1) :], "seq", 1)
    extended = jnp.concatenate([earlier, projected], axis=0).astype(jnp.float32)
    mixed = short_filter[0] * extended[taps - 1 :]
    for lag in range(1, taps):
        mixed = mixed + short_filter[lag] * extended[taps - 1 - lag : taps - 1 - lag + tok_rows]
    query = mixed[:, :width].astype(jnp.bfloat16)
    driven = (mixed[:, width : 2 * width] * mixed[:, 2 * width :]).astype(jnp.bfloat16)
    local_cols = inner // devices
    col_start = position * local_cols
    blocked = driven.reshape(tok_rows // inner, inner, width)
    piece = lax.all_to_all(blocked, "seq", split_axis=1, concat_axis=0, tiled=True)
    real_part, imag_part = rows_forward_first(piece, col_start, total)
    spec_real, spec_imag = rows_forward_second(
        (
            lax.all_to_all(
                real_part.astype(jnp.bfloat16), "seq", split_axis=0, concat_axis=1, tiled=True
            ).astype(real_part.dtype),
            lax.all_to_all(
                imag_part.astype(jnp.bfloat16), "seq", split_axis=0, concat_axis=1, tiled=True
            ).astype(imag_part.dtype),
        )
    )
    resident = jnp.transpose(spectra, (0, 2, 3, 1))
    prod_real, prod_imag = apply_filter(spec_real, spec_imag, resident)
    local_rows = outer // devices
    back_real, back_imag = rows_inverse_second(prod_real, prod_imag, position * local_rows, total)
    response_cols = rows_inverse_first(
        (
            lax.all_to_all(
                as_sent(back_real), "seq", split_axis=1, concat_axis=0, tiled=True
            ).astype(back_real.dtype),
            lax.all_to_all(
                as_sent(back_imag), "seq", split_axis=1, concat_axis=0, tiled=True
            ).astype(back_imag.dtype),
        ),
        total,
    )
    response_cols = response_cols + skip_gain[None, None, :] * piece.astype(jnp.float32)
    response = lax.all_to_all(
        response_cols, "seq", split_axis=0, concat_axis=1, tiled=True
    ).reshape(tok_rows, width)
    gated = (query.astype(jnp.float32) * response).astype(jnp.bfloat16)
    hidden_state = (
        tokens.astype(jnp.float32) + jnp.dot(gated, out_weight, preferred_element_type=jnp.float32)
    ).astype(jnp.bfloat16)
    second_norm = rms_scale(hidden_state, mlp_gain).astype(jnp.bfloat16)
    activated = jax.nn.gelu(
        jnp.dot(second_norm, up_weight, preferred_element_type=jnp.float32), approximate=True
    ).astype(jnp.bfloat16)
    return (
        hidden_state.astype(jnp.float32)
        + jnp.dot(activated, down_weight, preferred_element_type=jnp.float32)
    ).astype(jnp.bfloat16)


MESH = pl.DeviceIdType.MESH


def dft_tables(n, outer, inner, groups, share):
    kl = outer // n
    k1 = np.arange(outer)
    ang = 2.0 * np.pi * (np.outer(k1, np.arange(n)) % outer) / outer
    weights = np.stack([np.cos(ang), -np.sin(ang)]).reshape(2, n, kl, n)
    first = np.einsum("rpkn,gh,ij->rgpiknhj", weights, np.eye(groups), np.eye(share))
    first = first.reshape(2 * groups * outer * share, n * groups * share)
    ang = 2.0 * np.pi * (np.outer(np.arange(inner), np.arange(inner)) % inner) / inner
    cos, sin = np.cos(ang), np.sin(ang)
    second = np.block([[cos, -sin], [sin, cos]])
    ang = 2.0 * np.pi * np.outer(k1, np.arange(inner)) / (outer * inner)
    turn = np.stack([np.cos(ang), np.sin(ang)]).reshape(2, n, 1, kl, inner)
    turn = np.broadcast_to(turn, (2, n, share, kl, inner)).reshape(2, n * share * kl, inner)
    low = lambda a: a.astype(ml_dtypes.bfloat16)
    return low(first), low(np.ascontiguousarray(first.T)), low(second), turn.astype(np.float32)


def kernel(
    groups, n, share,
    tokens_hbm, norm_hbm, in_hbm, short_hbm, skip_hbm, mlp_hbm,
    spectra, out_hbm, up_hbm, down_hbm, first_hbm, last_hbm, second_hbm, turn_hbm,
    result,
    tokens, norm_gain, in_weight, short_filter, skip_gain, mlp_gain,
    filt, halo, extended, sent, signal, back, response,
    out_weight, up_weight, down_weight, first, last, second, turn,
    local_sem, filt_send, filt_recv, halo_send, halo_recv,
    sig_send, sig_recv, resp_send, resp_recv,
):
    count = groups * n
    group = lax.axis_index("groups")
    position = lax.axis_index("seq")
    me = position * groups + group
    rows, width = tokens.shape
    taps = short_filter.shape[0]

    def place(index):
        return (lax.rem(index, groups), lax.div(index, groups))

    barrier = pltpu.get_barrier_semaphore()

    def greet(step, carry):
        pl.semaphore_signal(
            barrier, inc=1, device_id=place(lax.rem(me + step, count)), device_id_type=MESH
        )
        return carry

    lax.fori_loop(1, count, greet, 0)

    early = (
        (tokens_hbm, tokens), (norm_hbm, norm_gain), (in_hbm, in_weight),
        (short_hbm, short_filter),
    )
    pairs = early + (
        (first_hbm, first), (second_hbm, second), (turn_hbm, turn), (last_hbm, last),
        (out_hbm, out_weight), (up_hbm, up_weight), (down_hbm, down_weight),
        (skip_hbm, skip_gain), (mlp_hbm, mlp_gain),
    )
    loads = [
        pltpu.make_async_copy(source, target, local_sem.at[i])
        for i, (source, target) in enumerate(pairs)
    ]

    def channels(seq_index):
        return pl.ds((seq_index * groups + group) * share, share)

    own_filter = pltpu.make_async_copy(
        spectra.at[:, channels(position)], filt.at[position], local_sem.at[len(pairs)]
    )

    def filter_copy(target, source):
        return pltpu.make_async_remote_copy(
            src_ref=spectra.at[:, channels(target)], dst_ref=filt.at[source],
            send_sem=filt_send.at[target], recv_sem=filt_recv.at[source],
            device_id=(group, target), device_id_type=MESH,
        )

    def halo_copy(target):
        return pltpu.make_async_remote_copy(
            src_ref=tokens_hbm.at[pl.ds(rows - 16, 16)], dst_ref=halo,
            send_sem=halo_send.at[0], recv_sem=halo_recv.at[0],
            device_id=(group, target), device_id_type=MESH,
        )

    def signal_copy(target, source):
        return pltpu.make_async_remote_copy(
            src_ref=sent.at[target], dst_ref=signal.at[source],
            send_sem=sig_send.at[target], recv_sem=sig_recv.at[source],
            device_id=place(target), device_id_type=MESH,
        )

    def response_copy(target, source):
        return pltpu.make_async_remote_copy(
            src_ref=back.at[target], dst_ref=response.at[source],
            send_sem=resp_send.at[target], recv_sem=resp_recv.at[source],
            device_id=place(target), device_id_type=MESH,
        )

    def each(total, own, action):
        def body(step, carry):
            action(lax.rem(own + step, total))
            return carry

        lax.fori_loop(1, total, body, 0)

    for load in loads:
        load.start()
    own_filter.start()
    pl.semaphore_wait(barrier, count - 1)

    @pl.when(position < n - 1)
    def _():
        halo_copy(position + 1).start()

    @pl.when(position == 0)
    def _():
        halo[...] = jnp.zeros_like(halo)

    each(n, position, lambda other: filter_copy(other, position).start())

    for load in loads[: len(early)]:
        load.wait()
    gain = norm_gain[...].reshape(1, width)
    weight = in_weight[...]

    def project(values):
        normed = rms_scale(values, gain).astype(jnp.bfloat16)
        made = jnp.dot(normed, weight, preferred_element_type=jnp.float32)
        return made.astype(jnp.bfloat16).astype(jnp.float32)

    extended[pl.ds(8, rows), :] = project(tokens[...])

    @pl.when(position > 0)
    def _():
        halo_copy(position).wait_recv()

    extended[pl.ds(0, 8), :] = project(halo[...])[8:, :]
    mixed = short_filter[0:1, :] * extended[pl.ds(8, rows), :]
    for lag in range(1, taps):
        mixed = mixed + short_filter[lag : lag + 1, :] * extended[pl.ds(8 - lag, rows), :]
    query = mixed[:, :width].astype(jnp.bfloat16).astype(jnp.float32)
    driven = (mixed[:, width : 2 * width] * mixed[:, 2 * width :]).astype(jnp.bfloat16)
    driven = driven.astype(jnp.float32)
    sent[...] = driven.T.reshape(count, share, rows).astype(jnp.bfloat16)
    each(count, me, lambda other: signal_copy(other, me).start())
    signal[pl.ds(me, 1)] = sent[pl.ds(me, 1)]

    for load in loads[len(early) :]:
        load.wait()
    own_filter.wait()
    each(count, me, lambda other: signal_copy(me, other).wait_recv())

    half = groups * n * share * (filt.shape[3])
    bins = half // groups
    gathered = signal[...].astype(jnp.float32).reshape(count * share, rows).astype(jnp.bfloat16)
    part = jnp.dot(first[...], gathered, preferred_element_type=jnp.float32)
    part_real = part[:half].reshape(groups, bins, rows)
    part_imag = part[half:].reshape(groups, bins, rows)
    turn_cos, turn_sin = turn[0][None], turn[1][None]
    turned = jnp.concatenate(
        [part_real * turn_cos + part_imag * turn_sin, part_imag * turn_cos - part_real * turn_sin],
        axis=-1,
    ).reshape(half, 2 * rows).astype(jnp.bfloat16)
    spec = jnp.dot(turned, second[...], preferred_element_type=jnp.float32)
    spec_real = spec[:, :rows].reshape(groups, bins, rows)
    spec_imag = spec[:, rows:].reshape(groups, bins, rows)
    each(n, position, lambda other: filter_copy(position, other).wait_recv())
    filt_real = filt[:, 0].astype(jnp.float32).reshape(1, bins, rows)
    filt_imag = filt[:, 1].astype(jnp.float32).reshape(1, bins, rows)
    product = jnp.concatenate(
        [
            spec_real * filt_real - spec_imag * filt_imag,
            -(spec_real * filt_imag + spec_imag * filt_real),
        ],
        axis=-1,
    ).reshape(half, 2 * rows).astype(jnp.bfloat16)
    inner_back = jnp.dot(product, second[...], preferred_element_type=jnp.float32)
    back_real = inner_back[:, :rows].reshape(groups, bins, rows)
    back_imag = inner_back[:, rows:].reshape(groups, bins, rows)
    turned_back = jnp.concatenate(
        [
            (back_real * turn_cos + back_imag * turn_sin).reshape(half, rows),
            (back_real * turn_sin - back_imag * turn_cos).reshape(half, rows),
        ],
        axis=0,
    ).astype(jnp.bfloat16)
    total = 2 * n * rows
    conv = jnp.dot(last[...], turned_back, preferred_element_type=jnp.float32) * (1.0 / total)
    back[...] = conv.reshape(count, share, rows).astype(jnp.bfloat16)
    each(count, me, lambda other: response_copy(other, me).start())
    response[pl.ds(me, 1)] = back[pl.ds(me, 1)]
    each(count, me, lambda other: response_copy(me, other).wait_recv())

    answer = response[...].astype(jnp.float32).reshape(width, rows).T
    answer = answer + skip_gain[...].reshape(1, width) * driven
    gated = (query * answer).astype(jnp.bfloat16)
    hidden = (
        tokens[...].astype(jnp.float32)
        + jnp.dot(gated, out_weight[...], preferred_element_type=jnp.float32)
    ).astype(jnp.bfloat16)
    second_norm = rms_scale(hidden, mlp_gain[...].reshape(1, width)).astype(jnp.bfloat16)
    activated = jax.nn.gelu(
        jnp.dot(second_norm, up_weight[...], preferred_element_type=jnp.float32), approximate=True
    ).astype(jnp.bfloat16)
    result[...] = (
        hidden.astype(jnp.float32)
        + jnp.dot(activated, down_weight[...], preferred_element_type=jnp.float32)
    ).astype(jnp.bfloat16)

    @pl.when(position < n - 1)
    def _():
        halo_copy(position + 1).wait_send()

    each(n, position, lambda other: filter_copy(other, position).wait_send())
    each(count, me, lambda other: signal_copy(other, me).wait_send())
    each(count, me, lambda other: response_copy(other, me).wait_send())


def fused(
    tokens, norm_gain, in_weight, short_filter, spectra, skip_gain,
    out_weight, mlp_gain, up_weight, down_weight,
):
    rows, width = tokens.shape
    groups, n = lax.axis_size("groups"), lax.axis_size("seq")
    count = groups * n
    share = width // count
    local_outer = spectra.shape[2]
    first, last, second, turn = dft_tables(n, n * local_outer, rows, groups, share)
    low = jnp.bfloat16
    vmem = pl.BlockSpec(memory_space=pltpu.VMEM)
    far = pl.BlockSpec(memory_space=pltpu.HBM)
    dma = pltpu.SemaphoreType.DMA
    small = [tokens, norm_gain, in_weight, short_filter, skip_gain, mlp_gain]
    held = [out_weight, up_weight, down_weight, first, last, second, turn]
    return pl.pallas_call(
        functools.partial(kernel, groups, n, share),
        out_shape=jax.ShapeDtypeStruct((rows, width), low),
        in_specs=[far] * 14,
        out_specs=vmem,
        scratch_shapes=[pltpu.VMEM(a.shape, a.dtype) for a in small]
        + [
            pltpu.VMEM((n, 2, share, local_outer, rows), low),
            pltpu.VMEM((16, width), low),
            pltpu.VMEM((rows + 8, 3 * width), jnp.float32),
            pltpu.VMEM((count, share, rows), low),
            pltpu.VMEM((count, share, rows), low),
            pltpu.VMEM((count, share, rows), low),
            pltpu.VMEM((count, share, rows), low),
        ]
        + [pltpu.VMEM(a.shape, a.dtype) for a in held]
        + [
            dma((16,)), dma((n,)), dma((n,)), dma((1,)), dma((1,)),
            dma((count,)), dma((count,)), dma((count,)), dma((count,)),
        ],
        compiler_params=pltpu.CompilerParams(
            collective_id=0, has_side_effects=True, vmem_limit_bytes=64 * 1024 * 1024
        ),
    )(
        tokens, norm_gain, in_weight, short_filter, skip_gain, mlp_gain,
        spectra, out_weight, up_weight, down_weight, first, last, second, turn,
    )


def solution(mesh):
    in_specs = (
        P(("groups", "seq"), None),
        P(),
        P(),
        P(),
        P(None, None, "seq", None),
        P(),
        P(),
        P(),
        P(),
        P(),
    )
    out_specs = P(("groups", "seq"), None)

    def layer(*args):
        rows, width = args[0].shape
        spectra = args[4]
        fits = (
            width % (8 * mesh.size) == 0
            and rows == spectra.shape[3]
            and spectra.shape[2] == 2
            and rows % 128 == 0
        )
        return (fused if fits else local)(*args)

    return jax.shard_map(layer, mesh=mesh, in_specs=in_specs, out_specs=out_specs, check_vma=False)
```

```python
import functools
import math

import jax
import jax.numpy as jnp
import ml_dtypes
import numpy as np
from jax import lax
from jax.experimental import pallas as pl
from jax.experimental.pallas import tpu as pltpu
from jax.sharding import PartitionSpec as P

exact = lax.Precision.HIGHEST
epsilon = 1e-06


def passed_along(value, axis, steps):
    count = lax.axis_size(axis)
    first, last = (max(0, -steps), min(count, count - steps))
    return lax.ppermute(value, axis, [(source, source + steps) for source in range(first, last)])


def as_sent(array):
    return jax.tree.map(lambda a: a.astype(jnp.bfloat16) if a.dtype == jnp.float32 else a, array)


def rms_scale(values, gain):
    wide = values.astype(jnp.float32)
    return wide * lax.rsqrt(jnp.mean(wide * wide, axis=-1, keepdims=True) + epsilon) * gain


def phase_table(out_start, out_count, in_start, in_count, period):
    index_out = out_start + lax.iota(jnp.int32, out_count)[:, None]
    index_in = in_start + lax.iota(jnp.int32, in_count)[None, :]
    angle = 2.0 * math.pi / period * (index_out * index_in % period).astype(jnp.float32)
    return (jnp.cos(angle), jnp.sin(angle))


def apply_filter(spec_real, spec_imag, filt):
    filt_real = filt[0].astype(jnp.float32)
    filt_imag = filt[1].astype(jnp.float32)
    return (
        spec_real * filt_real - spec_imag * filt_imag,
        spec_real * filt_imag + spec_imag * filt_real,
    )


def rows_forward_first(piece, column_start, total):
    half = piece.shape[0]
    length = 2 * half
    count = piece.shape[1]
    cosine, sine = phase_table(0, length, 0, half, length)
    wide = piece.astype(jnp.float32)
    real_part = jnp.einsum("kn,nmc->kmc", cosine, wide, precision=exact)
    imag_part = -jnp.einsum("kn,nmc->kmc", sine, wide, precision=exact)
    turn_cos, turn_sin = phase_table(0, length, column_start, count, total)
    turn_cos = turn_cos[:, :, None]
    turn_sin = turn_sin[:, :, None]
    return (
        real_part * turn_cos + imag_part * turn_sin,
        imag_part * turn_cos - real_part * turn_sin,
    )


def rows_forward_second(parts):
    real_part, imag_part = parts
    size = real_part.shape[1]
    cosine, sine = phase_table(0, size, 0, size, size)
    real_cos = jnp.einsum("kn,anc->akc", cosine, real_part, precision=exact)
    real_sin = jnp.einsum("kn,anc->akc", sine, real_part, precision=exact)
    imag_cos = jnp.einsum("kn,anc->akc", cosine, imag_part, precision=exact)
    imag_sin = jnp.einsum("kn,anc->akc", sine, imag_part, precision=exact)
    return (real_cos + imag_sin, imag_cos - real_sin)


def rows_inverse_second(real_part, imag_part, row_start, total):
    rows = real_part.shape[0]
    size = real_part.shape[1]
    cosine, sine = phase_table(0, size, 0, size, size)
    real_cos = jnp.einsum("nk,akc->anc", cosine, real_part, precision=exact)
    real_sin = jnp.einsum("nk,akc->anc", sine, real_part, precision=exact)
    imag_cos = jnp.einsum("nk,akc->anc", cosine, imag_part, precision=exact)
    imag_sin = jnp.einsum("nk,akc->anc", sine, imag_part, precision=exact)
    out_real = real_cos - imag_sin
    out_imag = real_sin + imag_cos
    turn_cos, turn_sin = phase_table(row_start, rows, 0, size, total)
    turn_cos = turn_cos[:, :, None]
    turn_sin = turn_sin[:, :, None]
    return (out_real * turn_cos - out_imag * turn_sin, out_real * turn_sin + out_imag * turn_cos)


def rows_inverse_first(parts, total):
    real_part, imag_part = parts
    length = real_part.shape[0]
    half = length // 2
    cosine, sine = phase_table(0, half, 0, length, length)
    summed = jnp.einsum("nk,kmc->nmc", cosine, real_part, precision=exact) - jnp.einsum(
        "nk,kmc->nmc", sine, imag_part, precision=exact
    )
    return summed / total


def local(
    tokens,
    norm_gain,
    in_weight,
    short_filter,
    spectra,
    skip_gain,
    out_weight,
    mlp_gain,
    up_weight,
    down_weight,
):
    tok_rows, width = tokens.shape
    devices = lax.axis_size("seq")
    position = lax.axis_index("seq")
    total = 2 * tok_rows * devices
    inner = min(tok_rows, 512)
    outer = total // inner
    normed = rms_scale(tokens, norm_gain).astype(jnp.bfloat16)
    projected = jnp.dot(normed, in_weight, preferred_element_type=jnp.float32).astype(jnp.bfloat16)
    taps = short_filter.shape[0]
    earlier = passed_along(projected[tok_rows - (taps - 1) :], "seq", 1)
    extended = jnp.concatenate([earlier, projected], axis=0).astype(jnp.float32)
    mixed = short_filter[0] * extended[taps - 1 :]
    for lag in range(1, taps):
        mixed = mixed + short_filter[lag] * extended[taps - 1 - lag : taps - 1 - lag + tok_rows]
    query = mixed[:, :width].astype(jnp.bfloat16)
    driven = (mixed[:, width : 2 * width] * mixed[:, 2 * width :]).astype(jnp.bfloat16)
    local_cols = inner // devices
    col_start = position * local_cols
    blocked = driven.reshape(tok_rows // inner, inner, width)
    piece = lax.all_to_all(blocked, "seq", split_axis=1, concat_axis=0, tiled=True)
    real_part, imag_part = rows_forward_first(piece, col_start, total)
    spec_real, spec_imag = rows_forward_second(
        (
            lax.all_to_all(
                real_part.astype(jnp.bfloat16), "seq", split_axis=0, concat_axis=1, tiled=True
            ).astype(real_part.dtype),
            lax.all_to_all(
                imag_part.astype(jnp.bfloat16), "seq", split_axis=0, concat_axis=1, tiled=True
            ).astype(imag_part.dtype),
        )
    )
    resident = jnp.transpose(spectra, (0, 2, 3, 1))
    prod_real, prod_imag = apply_filter(spec_real, spec_imag, resident)
    local_rows = outer // devices
    back_real, back_imag = rows_inverse_second(prod_real, prod_imag, position * local_rows, total)
    response_cols = rows_inverse_first(
        (
            lax.all_to_all(
                as_sent(back_real), "seq", split_axis=1, concat_axis=0, tiled=True
            ).astype(back_real.dtype),
            lax.all_to_all(
                as_sent(back_imag), "seq", split_axis=1, concat_axis=0, tiled=True
            ).astype(back_imag.dtype),
        ),
        total,
    )
    response_cols = response_cols + skip_gain[None, None, :] * piece.astype(jnp.float32)
    response = lax.all_to_all(
        response_cols, "seq", split_axis=0, concat_axis=1, tiled=True
    ).reshape(tok_rows, width)
    gated = (query.astype(jnp.float32) * response).astype(jnp.bfloat16)
    hidden_state = (
        tokens.astype(jnp.float32) + jnp.dot(gated, out_weight, preferred_element_type=jnp.float32)
    ).astype(jnp.bfloat16)
    second_norm = rms_scale(hidden_state, mlp_gain).astype(jnp.bfloat16)
    activated = jax.nn.gelu(
        jnp.dot(second_norm, up_weight, preferred_element_type=jnp.float32), approximate=True
    ).astype(jnp.bfloat16)
    return (
        hidden_state.astype(jnp.float32)
        + jnp.dot(activated, down_weight, preferred_element_type=jnp.float32)
    ).astype(jnp.bfloat16)


MESH = pl.DeviceIdType.MESH


def dft_tables(n, outer, inner, groups, share):
    kl = outer // n
    k1 = np.arange(outer)
    ang = 2.0 * np.pi * (np.outer(k1, np.arange(n)) % outer) / outer
    weights = np.stack([np.cos(ang), -np.sin(ang)]).reshape(2, n, kl, n)
    first = np.einsum("rpkn,gh,ij->rgpiknhj", weights, np.eye(groups), np.eye(share))
    first = first.reshape(2 * groups * outer * share, n * groups * share)
    ang = 2.0 * np.pi * (np.outer(np.arange(inner), np.arange(inner)) % inner) / inner
    cos, sin = np.cos(ang), np.sin(ang)
    second = np.block([[cos, -sin], [sin, cos]])
    ang = 2.0 * np.pi * np.outer(k1, np.arange(inner)) / (outer * inner)
    turn = np.stack([np.cos(ang), np.sin(ang)]).reshape(2, n, 1, kl, inner)
    turn = np.broadcast_to(turn, (2, n, share, kl, inner)).reshape(2, n * share * kl, inner)
    low = lambda a: a.astype(ml_dtypes.bfloat16)
    return low(first), low(np.ascontiguousarray(first.T)), low(second), turn.astype(np.float32)


def kernel(
    groups, n, share,
    tokens_hbm, norm_hbm, in_hbm, short_hbm, skip_hbm, mlp_hbm,
    spectra, out_hbm, up_hbm, down_hbm, first_hbm, last_hbm, second_hbm, turn_hbm,
    result,
    tokens, norm_gain, in_weight, short_filter, skip_gain, mlp_gain,
    filt, halo, extended, sent, signal, back, response,
    out_weight, up_weight, down_weight, first, last, second, turn,
    local_sem, filt_send, filt_recv, halo_send, halo_recv,
    sig_send, sig_recv, resp_send, resp_recv,
):
    count = groups * n
    group = lax.axis_index("groups")
    position = lax.axis_index("seq")
    me = position * groups + group
    rows, width = tokens.shape
    taps = short_filter.shape[0]

    def place(index):
        return (lax.rem(index, groups), lax.div(index, groups))

    barrier = pltpu.get_barrier_semaphore()

    def greet(step, carry):
        pl.semaphore_signal(
            barrier, inc=1, device_id=place(lax.rem(me + step, count)), device_id_type=MESH
        )
        return carry

    lax.fori_loop(1, count, greet, 0, unroll=True)

    early = (
        (tokens_hbm, tokens), (norm_hbm, norm_gain), (in_hbm, in_weight),
        (short_hbm, short_filter),
    )
    pairs = early + (
        (first_hbm, first), (second_hbm, second), (turn_hbm, turn), (last_hbm, last),
        (out_hbm, out_weight), (up_hbm, up_weight), (down_hbm, down_weight),
        (skip_hbm, skip_gain), (mlp_hbm, mlp_gain),
    )
    loads = [
        pltpu.make_async_copy(source, target, local_sem.at[i])
        for i, (source, target) in enumerate(pairs)
    ]

    def channels(seq_index):
        return pl.ds((seq_index * groups + group) * share, share)

    own_filter = pltpu.make_async_copy(
        spectra.at[:, channels(position)], filt.at[position], local_sem.at[len(pairs)]
    )

    def filter_copy(target, source):
        return pltpu.make_async_remote_copy(
            src_ref=spectra.at[:, channels(target)], dst_ref=filt.at[source],
            send_sem=filt_send.at[0], recv_sem=filt_recv.at[0],
            device_id=(group, target), device_id_type=MESH,
        )

    def halo_copy(target):
        return pltpu.make_async_remote_copy(
            src_ref=tokens_hbm.at[pl.ds(rows - 16, 16)], dst_ref=halo,
            send_sem=halo_send.at[0], recv_sem=halo_recv.at[0],
            device_id=(group, target), device_id_type=MESH,
        )

    def signal_copy(target, source):
        return pltpu.make_async_remote_copy(
            src_ref=sent.at[target], dst_ref=signal.at[source],
            send_sem=sig_send.at[0], recv_sem=sig_recv.at[0],
            device_id=place(target), device_id_type=MESH,
        )

    def response_copy(target, source):
        return pltpu.make_async_remote_copy(
            src_ref=back.at[target], dst_ref=response.at[source],
            send_sem=resp_send.at[0], recv_sem=resp_recv.at[0],
            device_id=place(target), device_id_type=MESH,
        )

    def all_of(landed, send_sem, recv_sem):
        blocks = landed.at[pl.ds(0, landed.shape[0] - 1)]
        return pltpu.make_async_remote_copy(
            src_ref=blocks, dst_ref=blocks, send_sem=send_sem.at[0], recv_sem=recv_sem.at[0],
            device_id=place(lax.rem(me + groups, count)), device_id_type=MESH,
        )

    def each(total, own, action):
        def body(step, carry):
            action(lax.rem(own + step, total))
            return carry

        lax.fori_loop(1, total, body, 0, unroll=True)

    for load in loads:
        load.start()
    own_filter.start()
    pl.semaphore_wait(barrier, count - 1)

    @pl.when(position < n - 1)
    def _():
        halo_copy(position + 1).start()

    @pl.when(position == 0)
    def _():
        halo[...] = jnp.zeros_like(halo)

    each(n, position, lambda other: filter_copy(other, position).start())

    for load in loads[: len(early)]:
        load.wait()
    gain = norm_gain[...].reshape(1, width)
    weight = in_weight[...]

    def project(values):
        normed = rms_scale(values, gain).astype(jnp.bfloat16)
        made = jnp.dot(normed, weight, preferred_element_type=jnp.float32)
        return made.astype(jnp.bfloat16).astype(jnp.float32)

    extended[pl.ds(8, rows), :] = project(tokens[...])

    @pl.when(position > 0)
    def _():
        halo_copy(position).wait_recv()

    extended[pl.ds(0, 8), :] = project(halo[...])[8:, :]
    mixed = short_filter[0:1, :] * extended[pl.ds(8, rows), :]
    for lag in range(1, taps):
        mixed = mixed + short_filter[lag : lag + 1, :] * extended[pl.ds(8 - lag, rows), :]
    query = mixed[:, :width].astype(jnp.bfloat16).astype(jnp.float32)
    driven = (mixed[:, width : 2 * width] * mixed[:, 2 * width :]).astype(jnp.bfloat16)
    driven = driven.astype(jnp.float32)
    sent[...] = driven.T.reshape(count, share, rows).astype(jnp.bfloat16)
    each(count, me, lambda other: signal_copy(other, me).start())
    signal[pl.ds(me, 1)] = sent[pl.ds(me, 1)]

    for load in loads[len(early) :]:
        load.wait()
    own_filter.wait()
    all_of(signal, sig_send, sig_recv).wait_recv()

    half = groups * n * share * (filt.shape[3])
    bins = half // groups
    gathered = signal[...].astype(jnp.float32).reshape(count * share, rows).astype(jnp.bfloat16)
    part = jnp.dot(first[...], gathered, preferred_element_type=jnp.float32)
    part_real = part[:half].reshape(groups, bins, rows)
    part_imag = part[half:].reshape(groups, bins, rows)
    turn_cos, turn_sin = turn[0][None], turn[1][None]
    turned = jnp.concatenate(
        [part_real * turn_cos + part_imag * turn_sin, part_imag * turn_cos - part_real * turn_sin],
        axis=-1,
    ).reshape(half, 2 * rows).astype(jnp.bfloat16)
    spec = jnp.dot(turned, second[...], preferred_element_type=jnp.float32)
    spec_real = spec[:, :rows].reshape(groups, bins, rows)
    spec_imag = spec[:, rows:].reshape(groups, bins, rows)
    all_of(filt, filt_send, filt_recv).wait_recv()
    filt_real = filt[:, 0].astype(jnp.float32).reshape(1, bins, rows)
    filt_imag = filt[:, 1].astype(jnp.float32).reshape(1, bins, rows)
    product = jnp.concatenate(
        [
            spec_real * filt_real - spec_imag * filt_imag,
            -(spec_real * filt_imag + spec_imag * filt_real),
        ],
        axis=-1,
    ).reshape(half, 2 * rows).astype(jnp.bfloat16)
    inner_back = jnp.dot(product, second[...], preferred_element_type=jnp.float32)
    back_real = inner_back[:, :rows].reshape(groups, bins, rows)
    back_imag = inner_back[:, rows:].reshape(groups, bins, rows)
    turned_back = jnp.concatenate(
        [
            (back_real * turn_cos + back_imag * turn_sin).reshape(half, rows),
            (back_real * turn_sin - back_imag * turn_cos).reshape(half, rows),
        ],
        axis=0,
    ).astype(jnp.bfloat16)
    total = 2 * n * rows
    conv = jnp.dot(last[...], turned_back, preferred_element_type=jnp.float32) * (1.0 / total)
    back[...] = conv.reshape(count, share, rows).astype(jnp.bfloat16)
    each(count, me, lambda other: response_copy(other, me).start())
    response[pl.ds(me, 1)] = back[pl.ds(me, 1)]
    all_of(response, resp_send, resp_recv).wait_recv()

    answer = response[...].astype(jnp.float32).reshape(width, rows).T
    answer = answer + skip_gain[...].reshape(1, width) * driven
    gated = (query * answer).astype(jnp.bfloat16)
    hidden = (
        tokens[...].astype(jnp.float32)
        + jnp.dot(gated, out_weight[...], preferred_element_type=jnp.float32)
    ).astype(jnp.bfloat16)
    second_norm = rms_scale(hidden, mlp_gain[...].reshape(1, width)).astype(jnp.bfloat16)
    activated = jax.nn.gelu(
        jnp.dot(second_norm, up_weight[...], preferred_element_type=jnp.float32), approximate=True
    ).astype(jnp.bfloat16)
    result[...] = (
        hidden.astype(jnp.float32)
        + jnp.dot(activated, down_weight[...], preferred_element_type=jnp.float32)
    ).astype(jnp.bfloat16)

    @pl.when(position < n - 1)
    def _():
        halo_copy(position + 1).wait_send()

    all_of(filt, filt_send, filt_recv).wait_send()
    all_of(signal, sig_send, sig_recv).wait_send()
    all_of(response, resp_send, resp_recv).wait_send()


def fused(
    tokens, norm_gain, in_weight, short_filter, spectra, skip_gain,
    out_weight, mlp_gain, up_weight, down_weight,
):
    rows, width = tokens.shape
    groups, n = lax.axis_size("groups"), lax.axis_size("seq")
    count = groups * n
    share = width // count
    local_outer = spectra.shape[2]
    first, last, second, turn = dft_tables(n, n * local_outer, rows, groups, share)
    low = jnp.bfloat16
    vmem = pl.BlockSpec(memory_space=pltpu.VMEM)
    far = pl.BlockSpec(memory_space=pltpu.HBM)
    dma = pltpu.SemaphoreType.DMA
    small = [tokens, norm_gain, in_weight, short_filter, skip_gain, mlp_gain]
    held = [out_weight, up_weight, down_weight, first, last, second, turn]
    return pl.pallas_call(
        functools.partial(kernel, groups, n, share),
        out_shape=pltpu.VMEM((rows, width), low),
        in_specs=[far] * 14,
        out_specs=vmem,
        scratch_shapes=[pltpu.VMEM(a.shape, a.dtype) for a in small]
        + [
            pltpu.VMEM((n, 2, share, local_outer, rows), low),
            pltpu.VMEM((16, width), low),
            pltpu.VMEM((rows + 8, 3 * width), jnp.float32),
            pltpu.VMEM((count, share, rows), low),
            pltpu.VMEM((count, share, rows), low),
            pltpu.VMEM((count, share, rows), low),
            pltpu.VMEM((count, share, rows), low),
        ]
        + [pltpu.VMEM(a.shape, a.dtype) for a in held]
        + [
            dma((16,)), dma((1,)), dma((1,)), dma((1,)), dma((1,)),
            dma((1,)), dma((1,)), dma((1,)), dma((1,)),
        ],
        compiler_params=pltpu.CompilerParams(
            collective_id=0, has_side_effects=True, vmem_limit_bytes=56 * 1024 * 1024
        ),
    )(
        tokens, norm_gain, in_weight, short_filter, skip_gain, mlp_gain,
        spectra, out_weight, up_weight, down_weight, first, last, second, turn,
    )


def solution(mesh):
    in_specs = (
        P(("groups", "seq"), None),
        P(),
        P(),
        P(),
        P(None, None, "seq", None),
        P(),
        P(),
        P(),
        P(),
        P(),
    )
    out_specs = P(("groups", "seq"), None)

    def layer(*args):
        rows, width = args[0].shape
        spectra = args[4]
        fits = (
            width % (8 * mesh.size) == 0
            and rows == spectra.shape[3]
            and spectra.shape[2] == 2
            and rows % 128 == 0
        )
        return (fused if fits else local)(*args)

    return jax.shard_map(layer, mesh=mesh, in_specs=in_specs, out_specs=out_specs, check_vma=False)
```

```python
import functools
import math

import jax
import jax.numpy as jnp
import ml_dtypes
import numpy as np
from jax import lax
from jax.experimental import pallas as pl
from jax.experimental.pallas import tpu as pltpu
from jax.sharding import PartitionSpec as P

exact = lax.Precision.HIGHEST
epsilon = 1e-06


def passed_along(value, axis, steps):
    count = lax.axis_size(axis)
    first, last = (max(0, -steps), min(count, count - steps))
    return lax.ppermute(value, axis, [(source, source + steps) for source in range(first, last)])


def as_sent(array):
    return jax.tree.map(lambda a: a.astype(jnp.bfloat16) if a.dtype == jnp.float32 else a, array)


def rms_scale(values, gain):
    wide = values.astype(jnp.float32)
    return wide * lax.rsqrt(jnp.mean(wide * wide, axis=-1, keepdims=True) + epsilon) * gain


def phase_table(out_start, out_count, in_start, in_count, period):
    index_out = out_start + lax.iota(jnp.int32, out_count)[:, None]
    index_in = in_start + lax.iota(jnp.int32, in_count)[None, :]
    angle = 2.0 * math.pi / period * (index_out * index_in % period).astype(jnp.float32)
    return (jnp.cos(angle), jnp.sin(angle))


def apply_filter(spec_real, spec_imag, filt):
    filt_real = filt[0].astype(jnp.float32)
    filt_imag = filt[1].astype(jnp.float32)
    return (
        spec_real * filt_real - spec_imag * filt_imag,
        spec_real * filt_imag + spec_imag * filt_real,
    )


def rows_forward_first(piece, column_start, total):
    half = piece.shape[0]
    length = 2 * half
    count = piece.shape[1]
    cosine, sine = phase_table(0, length, 0, half, length)
    wide = piece.astype(jnp.float32)
    real_part = jnp.einsum("kn,nmc->kmc", cosine, wide, precision=exact)
    imag_part = -jnp.einsum("kn,nmc->kmc", sine, wide, precision=exact)
    turn_cos, turn_sin = phase_table(0, length, column_start, count, total)
    turn_cos = turn_cos[:, :, None]
    turn_sin = turn_sin[:, :, None]
    return (
        real_part * turn_cos + imag_part * turn_sin,
        imag_part * turn_cos - real_part * turn_sin,
    )


def rows_forward_second(parts):
    real_part, imag_part = parts
    size = real_part.shape[1]
    cosine, sine = phase_table(0, size, 0, size, size)
    real_cos = jnp.einsum("kn,anc->akc", cosine, real_part, precision=exact)
    real_sin = jnp.einsum("kn,anc->akc", sine, real_part, precision=exact)
    imag_cos = jnp.einsum("kn,anc->akc", cosine, imag_part, precision=exact)
    imag_sin = jnp.einsum("kn,anc->akc", sine, imag_part, precision=exact)
    return (real_cos + imag_sin, imag_cos - real_sin)


def rows_inverse_second(real_part, imag_part, row_start, total):
    rows = real_part.shape[0]
    size = real_part.shape[1]
    cosine, sine = phase_table(0, size, 0, size, size)
    real_cos = jnp.einsum("nk,akc->anc", cosine, real_part, precision=exact)
    real_sin = jnp.einsum("nk,akc->anc", sine, real_part, precision=exact)
    imag_cos = jnp.einsum("nk,akc->anc", cosine, imag_part, precision=exact)
    imag_sin = jnp.einsum("nk,akc->anc", sine, imag_part, precision=exact)
    out_real = real_cos - imag_sin
    out_imag = real_sin + imag_cos
    turn_cos, turn_sin = phase_table(row_start, rows, 0, size, total)
    turn_cos = turn_cos[:, :, None]
    turn_sin = turn_sin[:, :, None]
    return (out_real * turn_cos - out_imag * turn_sin, out_real * turn_sin + out_imag * turn_cos)


def rows_inverse_first(parts, total):
    real_part, imag_part = parts
    length = real_part.shape[0]
    half = length // 2
    cosine, sine = phase_table(0, half, 0, length, length)
    summed = jnp.einsum("nk,kmc->nmc", cosine, real_part, precision=exact) - jnp.einsum(
        "nk,kmc->nmc", sine, imag_part, precision=exact
    )
    return summed / total


def local(
    tokens,
    norm_gain,
    in_weight,
    short_filter,
    spectra,
    skip_gain,
    out_weight,
    mlp_gain,
    up_weight,
    down_weight,
):
    tok_rows, width = tokens.shape
    devices = lax.axis_size("seq")
    position = lax.axis_index("seq")
    total = 2 * tok_rows * devices
    inner = min(tok_rows, 512)
    outer = total // inner
    normed = rms_scale(tokens, norm_gain).astype(jnp.bfloat16)
    projected = jnp.dot(normed, in_weight, preferred_element_type=jnp.float32).astype(jnp.bfloat16)
    taps = short_filter.shape[0]
    earlier = passed_along(projected[tok_rows - (taps - 1) :], "seq", 1)
    extended = jnp.concatenate([earlier, projected], axis=0).astype(jnp.float32)
    mixed = short_filter[0] * extended[taps - 1 :]
    for lag in range(1, taps):
        mixed = mixed + short_filter[lag] * extended[taps - 1 - lag : taps - 1 - lag + tok_rows]
    query = mixed[:, :width].astype(jnp.bfloat16)
    driven = (mixed[:, width : 2 * width] * mixed[:, 2 * width :]).astype(jnp.bfloat16)
    local_cols = inner // devices
    col_start = position * local_cols
    blocked = driven.reshape(tok_rows // inner, inner, width)
    piece = lax.all_to_all(blocked, "seq", split_axis=1, concat_axis=0, tiled=True)
    real_part, imag_part = rows_forward_first(piece, col_start, total)
    spec_real, spec_imag = rows_forward_second(
        (
            lax.all_to_all(
                real_part.astype(jnp.bfloat16), "seq", split_axis=0, concat_axis=1, tiled=True
            ).astype(real_part.dtype),
            lax.all_to_all(
                imag_part.astype(jnp.bfloat16), "seq", split_axis=0, concat_axis=1, tiled=True
            ).astype(imag_part.dtype),
        )
    )
    resident = jnp.transpose(spectra, (0, 2, 3, 1))
    prod_real, prod_imag = apply_filter(spec_real, spec_imag, resident)
    local_rows = outer // devices
    back_real, back_imag = rows_inverse_second(prod_real, prod_imag, position * local_rows, total)
    response_cols = rows_inverse_first(
        (
            lax.all_to_all(
                as_sent(back_real), "seq", split_axis=1, concat_axis=0, tiled=True
            ).astype(back_real.dtype),
            lax.all_to_all(
                as_sent(back_imag), "seq", split_axis=1, concat_axis=0, tiled=True
            ).astype(back_imag.dtype),
        ),
        total,
    )
    response_cols = response_cols + skip_gain[None, None, :] * piece.astype(jnp.float32)
    response = lax.all_to_all(
        response_cols, "seq", split_axis=0, concat_axis=1, tiled=True
    ).reshape(tok_rows, width)
    gated = (query.astype(jnp.float32) * response).astype(jnp.bfloat16)
    hidden_state = (
        tokens.astype(jnp.float32) + jnp.dot(gated, out_weight, preferred_element_type=jnp.float32)
    ).astype(jnp.bfloat16)
    second_norm = rms_scale(hidden_state, mlp_gain).astype(jnp.bfloat16)
    activated = jax.nn.gelu(
        jnp.dot(second_norm, up_weight, preferred_element_type=jnp.float32), approximate=True
    ).astype(jnp.bfloat16)
    return (
        hidden_state.astype(jnp.float32)
        + jnp.dot(activated, down_weight, preferred_element_type=jnp.float32)
    ).astype(jnp.bfloat16)


MESH = pl.DeviceIdType.MESH


def dft_tables(n, outer, inner, groups, share):
    kl = outer // n
    k1 = np.arange(outer)
    ang = 2.0 * np.pi * (np.outer(k1, np.arange(n)) % outer) / outer
    weights = np.stack([np.cos(ang), -np.sin(ang)]).reshape(2, n, kl, n)
    first = np.einsum("rpkn,gh,ij->rgpiknhj", weights, np.eye(groups), np.eye(share))
    first = first.reshape(2 * groups * outer * share, n * groups * share)
    ang = 2.0 * np.pi * (np.outer(np.arange(inner), np.arange(inner)) % inner) / inner
    cos, sin = np.cos(ang), np.sin(ang)
    second = np.block([[cos, -sin], [sin, cos]])
    ang = 2.0 * np.pi * np.outer(k1, np.arange(inner)) / (outer * inner)
    turn = np.stack([np.cos(ang), np.sin(ang)]).reshape(2, n, 1, kl, inner)
    turn = np.broadcast_to(turn, (2, n, share, kl, inner)).reshape(2, n * share * kl, inner)
    low = lambda a: a.astype(ml_dtypes.bfloat16)
    return low(first), low(np.ascontiguousarray(first.T)), low(second), turn.astype(np.float32)


def kernel(
    groups, n, share,
    tokens_hbm, norm_hbm, in_hbm, short_hbm, skip_hbm, mlp_hbm,
    spectra, out_hbm, up_hbm, down_hbm, first_hbm, last_hbm, second_hbm, turn_hbm,
    result,
    tokens, norm_gain, in_weight, short_filter, skip_gain, mlp_gain,
    filt, halo, extended, sent, signal, back, response,
    out_weight, up_weight, down_weight, first, last, second, turn,
    local_sem, filt_send, filt_recv, halo_send, halo_recv,
    sig_send, sig_recv, resp_send, resp_recv,
):
    count = groups * n
    group = lax.axis_index("groups")
    position = lax.axis_index("seq")
    me = position * groups + group
    rows, width = tokens.shape
    taps = short_filter.shape[0]

    def place(index):
        return (lax.rem(index, groups), lax.div(index, groups))

    barrier = pltpu.get_barrier_semaphore()

    def greet(step, carry):
        pl.semaphore_signal(
            barrier, inc=1, device_id=place(lax.rem(me + step, count)), device_id_type=MESH
        )
        return carry

    lax.fori_loop(1, count, greet, 0, unroll=True)

    early = (
        (tokens_hbm, tokens), (norm_hbm, norm_gain), (in_hbm, in_weight),
        (short_hbm, short_filter),
    )
    pairs = early + (
        (first_hbm, first), (second_hbm, second), (turn_hbm, turn), (last_hbm, last),
        (out_hbm, out_weight), (up_hbm, up_weight), (down_hbm, down_weight),
        (skip_hbm, skip_gain), (mlp_hbm, mlp_gain),
    )
    loads = [
        pltpu.make_async_copy(source, target, local_sem.at[i])
        for i, (source, target) in enumerate(pairs)
    ]

    def channels(seq_index):
        return pl.ds((seq_index * groups + group) * share, share)

    own_filter = pltpu.make_async_copy(
        spectra.at[:, channels(position)], filt.at[position], local_sem.at[len(pairs)]
    )

    def filter_copy(target, source):
        return pltpu.make_async_remote_copy(
            src_ref=spectra.at[:, channels(target)], dst_ref=filt.at[source],
            send_sem=filt_send.at[0], recv_sem=filt_recv.at[0],
            device_id=(group, target), device_id_type=MESH,
        )

    def halo_copy(target):
        return pltpu.make_async_remote_copy(
            src_ref=tokens_hbm.at[pl.ds(rows - 16, 16)], dst_ref=halo,
            send_sem=halo_send.at[0], recv_sem=halo_recv.at[0],
            device_id=(group, target), device_id_type=MESH,
        )

    def signal_copy(target, source):
        return pltpu.make_async_remote_copy(
            src_ref=sent.at[target], dst_ref=signal.at[source],
            send_sem=sig_send.at[0], recv_sem=sig_recv.at[0],
            device_id=place(target), device_id_type=MESH,
        )

    def response_copy(target, source):
        return pltpu.make_async_remote_copy(
            src_ref=back.at[target], dst_ref=response.at[source],
            send_sem=resp_send.at[0], recv_sem=resp_recv.at[0],
            device_id=place(target), device_id_type=MESH,
        )

    def all_of(landed, send_sem, recv_sem):
        blocks = landed.at[pl.ds(0, landed.shape[0] - 1)]
        return pltpu.make_async_remote_copy(
            src_ref=blocks, dst_ref=blocks, send_sem=send_sem.at[0], recv_sem=recv_sem.at[0],
            device_id=place(lax.rem(me + groups, count)), device_id_type=MESH,
        )

    def each(total, own, action):
        def body(step, carry):
            action(lax.rem(own + step, total))
            return carry

        lax.fori_loop(1, total, body, 0, unroll=True)

    for load in loads:
        load.start()
    own_filter.start()
    for load in loads[: len(early)]:
        load.wait()
    gain = norm_gain[...].reshape(1, width)
    weight = in_weight[...]

    def project(values):
        normed = rms_scale(values, gain).astype(jnp.bfloat16)
        made = jnp.dot(normed, weight, preferred_element_type=jnp.float32)
        return made.astype(jnp.bfloat16).astype(jnp.float32)

    extended[pl.ds(8, rows), :] = project(tokens[...])

    pl.semaphore_wait(barrier, count - 1)

    @pl.when(position < n - 1)
    def _():
        halo_copy(position + 1).start()

    @pl.when(position == 0)
    def _():
        halo[...] = jnp.zeros_like(halo)

    for step in range(1, (n + 1) // 2):
        filter_copy(lax.rem(position + step, n), position).start()

    @pl.when(position > 0)
    def _():
        halo_copy(position).wait_recv()

    extended[pl.ds(0, 8), :] = project(halo[...])[8:, :]
    mixed = short_filter[0:1, :] * extended[pl.ds(8, rows), :]
    for lag in range(1, taps):
        mixed = mixed + short_filter[lag : lag + 1, :] * extended[pl.ds(8 - lag, rows), :]
    query = mixed[:, :width].astype(jnp.bfloat16).astype(jnp.float32)
    driven = (mixed[:, width : 2 * width] * mixed[:, 2 * width :]).astype(jnp.bfloat16)
    driven = driven.astype(jnp.float32)
    sent[...] = driven.T.reshape(count, share, rows).astype(jnp.bfloat16)
    each(count, me, lambda other: signal_copy(other, me).start())
    for step in range((n + 1) // 2, n):
        filter_copy(lax.rem(position + step, n), position).start()
    signal[pl.ds(me, 1)] = sent[pl.ds(me, 1)]

    for load in loads[len(early) :]:
        load.wait()
    own_filter.wait()
    all_of(signal, sig_send, sig_recv).wait_recv()

    half = groups * n * share * (filt.shape[3])
    bins = half // groups
    gathered = signal[...].astype(jnp.float32).reshape(count * share, rows).astype(jnp.bfloat16)
    part = jnp.dot(first[...], gathered, preferred_element_type=jnp.float32)
    part_real = part[:half].reshape(groups, bins, rows)
    part_imag = part[half:].reshape(groups, bins, rows)
    turn_cos, turn_sin = turn[0][None], turn[1][None]
    turned = jnp.concatenate(
        [part_real * turn_cos + part_imag * turn_sin, part_imag * turn_cos - part_real * turn_sin],
        axis=-1,
    ).reshape(half, 2 * rows).astype(jnp.bfloat16)
    spec = jnp.dot(turned, second[...], preferred_element_type=jnp.float32)
    spec_real = spec[:, :rows].reshape(groups, bins, rows)
    spec_imag = spec[:, rows:].reshape(groups, bins, rows)
    all_of(filt, filt_send, filt_recv).wait_recv()
    filt_real = filt[:, 0].astype(jnp.float32).reshape(1, bins, rows)
    filt_imag = filt[:, 1].astype(jnp.float32).reshape(1, bins, rows)
    product = jnp.concatenate(
        [
            spec_real * filt_real - spec_imag * filt_imag,
            -(spec_real * filt_imag + spec_imag * filt_real),
        ],
        axis=-1,
    ).reshape(half, 2 * rows).astype(jnp.bfloat16)
    inner_back = jnp.dot(product, second[...], preferred_element_type=jnp.float32)
    back_real = inner_back[:, :rows].reshape(groups, bins, rows)
    back_imag = inner_back[:, rows:].reshape(groups, bins, rows)
    turned_back = jnp.concatenate(
        [
            (back_real * turn_cos + back_imag * turn_sin).reshape(half, rows),
            (back_real * turn_sin - back_imag * turn_cos).reshape(half, rows),
        ],
        axis=0,
    ).astype(jnp.bfloat16)
    total = 2 * n * rows
    conv = jnp.dot(last[...], turned_back, preferred_element_type=jnp.float32) * (1.0 / total)
    back[...] = conv.reshape(count, share, rows).astype(jnp.bfloat16)
    each(count, me, lambda other: response_copy(other, me).start())
    response[pl.ds(me, 1)] = back[pl.ds(me, 1)]
    all_of(response, resp_send, resp_recv).wait_recv()

    answer = response[...].astype(jnp.float32).reshape(width, rows).T
    answer = answer + skip_gain[...].reshape(1, width) * driven
    gated = (query * answer).astype(jnp.bfloat16)
    hidden = (
        tokens[...].astype(jnp.float32)
        + jnp.dot(gated, out_weight[...], preferred_element_type=jnp.float32)
    ).astype(jnp.bfloat16)
    second_norm = rms_scale(hidden, mlp_gain[...].reshape(1, width)).astype(jnp.bfloat16)
    activated = jax.nn.gelu(
        jnp.dot(second_norm, up_weight[...], preferred_element_type=jnp.float32), approximate=True
    ).astype(jnp.bfloat16)
    result[...] = (
        hidden.astype(jnp.float32)
        + jnp.dot(activated, down_weight[...], preferred_element_type=jnp.float32)
    ).astype(jnp.bfloat16)

    @pl.when(position < n - 1)
    def _():
        halo_copy(position + 1).wait_send()

    all_of(filt, filt_send, filt_recv).wait_send()
    all_of(signal, sig_send, sig_recv).wait_send()
    all_of(response, resp_send, resp_recv).wait_send()


def fused(
    tokens, norm_gain, in_weight, short_filter, spectra, skip_gain,
    out_weight, mlp_gain, up_weight, down_weight,
):
    rows, width = tokens.shape
    groups, n = lax.axis_size("groups"), lax.axis_size("seq")
    count = groups * n
    share = width // count
    local_outer = spectra.shape[2]
    first, last, second, turn = dft_tables(n, n * local_outer, rows, groups, share)
    low = jnp.bfloat16
    vmem = pl.BlockSpec(memory_space=pltpu.VMEM)
    far = pl.BlockSpec(memory_space=pltpu.HBM)
    dma = pltpu.SemaphoreType.DMA
    small = [tokens, norm_gain, in_weight, short_filter, skip_gain, mlp_gain]
    held = [out_weight, up_weight, down_weight, first, last, second, turn]
    return pl.pallas_call(
        functools.partial(kernel, groups, n, share),
        out_shape=pltpu.VMEM((rows, width), low),
        in_specs=[far] * 14,
        out_specs=vmem,
        scratch_shapes=[pltpu.VMEM(a.shape, a.dtype) for a in small]
        + [
            pltpu.VMEM((n, 2, share, local_outer, rows), low),
            pltpu.VMEM((16, width), low),
            pltpu.VMEM((rows + 8, 3 * width), jnp.float32),
            pltpu.VMEM((count, share, rows), low),
            pltpu.VMEM((count, share, rows), low),
            pltpu.VMEM((count, share, rows), low),
            pltpu.VMEM((count, share, rows), low),
        ]
        + [pltpu.VMEM(a.shape, a.dtype) for a in held]
        + [
            dma((16,)), dma((1,)), dma((1,)), dma((1,)), dma((1,)),
            dma((1,)), dma((1,)), dma((1,)), dma((1,)),
        ],
        compiler_params=pltpu.CompilerParams(
            collective_id=0, has_side_effects=True, vmem_limit_bytes=56 * 1024 * 1024
        ),
    )(
        tokens, norm_gain, in_weight, short_filter, skip_gain, mlp_gain,
        spectra, out_weight, up_weight, down_weight, first, last, second, turn,
    )


def solution(mesh):
    in_specs = (
        P(("groups", "seq"), None),
        P(),
        P(),
        P(),
        P(None, None, "seq", None),
        P(),
        P(),
        P(),
        P(),
        P(),
    )
    out_specs = P(("groups", "seq"), None)

    def layer(*args):
        rows, width = args[0].shape
        spectra = args[4]
        fits = (
            width % (8 * mesh.size) == 0
            and rows == spectra.shape[3]
            and spectra.shape[2] == 2
            and rows % 128 == 0
        )
        return (fused if fits else local)(*args)

    return jax.shard_map(layer, mesh=mesh, in_specs=in_specs, out_specs=out_specs, check_vma=False)
```

```python
import functools
import math

import jax
import jax.numpy as jnp
import ml_dtypes
import numpy as np
from jax import lax
from jax.experimental import pallas as pl
from jax.experimental.pallas import tpu as pltpu
from jax.sharding import PartitionSpec as P

exact = lax.Precision.HIGHEST
epsilon = 1e-06


def passed_along(value, axis, steps):
    count = lax.axis_size(axis)
    first, last = (max(0, -steps), min(count, count - steps))
    return lax.ppermute(value, axis, [(source, source + steps) for source in range(first, last)])


def as_sent(array):
    return jax.tree.map(lambda a: a.astype(jnp.bfloat16) if a.dtype == jnp.float32 else a, array)


def rms_scale(values, gain):
    wide = values.astype(jnp.float32)
    return wide * lax.rsqrt(jnp.mean(wide * wide, axis=-1, keepdims=True) + epsilon) * gain


def phase_table(out_start, out_count, in_start, in_count, period):
    index_out = out_start + lax.iota(jnp.int32, out_count)[:, None]
    index_in = in_start + lax.iota(jnp.int32, in_count)[None, :]
    angle = 2.0 * math.pi / period * (index_out * index_in % period).astype(jnp.float32)
    return (jnp.cos(angle), jnp.sin(angle))


def apply_filter(spec_real, spec_imag, filt):
    filt_real = filt[0].astype(jnp.float32)
    filt_imag = filt[1].astype(jnp.float32)
    return (
        spec_real * filt_real - spec_imag * filt_imag,
        spec_real * filt_imag + spec_imag * filt_real,
    )


def rows_forward_first(piece, column_start, total):
    half = piece.shape[0]
    length = 2 * half
    count = piece.shape[1]
    cosine, sine = phase_table(0, length, 0, half, length)
    wide = piece.astype(jnp.float32)
    real_part = jnp.einsum("kn,nmc->kmc", cosine, wide, precision=exact)
    imag_part = -jnp.einsum("kn,nmc->kmc", sine, wide, precision=exact)
    turn_cos, turn_sin = phase_table(0, length, column_start, count, total)
    turn_cos = turn_cos[:, :, None]
    turn_sin = turn_sin[:, :, None]
    return (
        real_part * turn_cos + imag_part * turn_sin,
        imag_part * turn_cos - real_part * turn_sin,
    )


def rows_forward_second(parts):
    real_part, imag_part = parts
    size = real_part.shape[1]
    cosine, sine = phase_table(0, size, 0, size, size)
    real_cos = jnp.einsum("kn,anc->akc", cosine, real_part, precision=exact)
    real_sin = jnp.einsum("kn,anc->akc", sine, real_part, precision=exact)
    imag_cos = jnp.einsum("kn,anc->akc", cosine, imag_part, precision=exact)
    imag_sin = jnp.einsum("kn,anc->akc", sine, imag_part, precision=exact)
    return (real_cos + imag_sin, imag_cos - real_sin)


def rows_inverse_second(real_part, imag_part, row_start, total):
    rows = real_part.shape[0]
    size = real_part.shape[1]
    cosine, sine = phase_table(0, size, 0, size, size)
    real_cos = jnp.einsum("nk,akc->anc", cosine, real_part, precision=exact)
    real_sin = jnp.einsum("nk,akc->anc", sine, real_part, precision=exact)
    imag_cos = jnp.einsum("nk,akc->anc", cosine, imag_part, precision=exact)
    imag_sin = jnp.einsum("nk,akc->anc", sine, imag_part, precision=exact)
    out_real = real_cos - imag_sin
    out_imag = real_sin + imag_cos
    turn_cos, turn_sin = phase_table(row_start, rows, 0, size, total)
    turn_cos = turn_cos[:, :, None]
    turn_sin = turn_sin[:, :, None]
    return (out_real * turn_cos - out_imag * turn_sin, out_real * turn_sin + out_imag * turn_cos)


def rows_inverse_first(parts, total):
    real_part, imag_part = parts
    length = real_part.shape[0]
    half = length // 2
    cosine, sine = phase_table(0, half, 0, length, length)
    summed = jnp.einsum("nk,kmc->nmc", cosine, real_part, precision=exact) - jnp.einsum(
        "nk,kmc->nmc", sine, imag_part, precision=exact
    )
    return summed / total


def local(
    tokens,
    norm_gain,
    in_weight,
    short_filter,
    spectra,
    skip_gain,
    out_weight,
    mlp_gain,
    up_weight,
    down_weight,
):
    tok_rows, width = tokens.shape
    devices = lax.axis_size("seq")
    position = lax.axis_index("seq")
    total = 2 * tok_rows * devices
    inner = min(tok_rows, 512)
    outer = total // inner
    normed = rms_scale(tokens, norm_gain).astype(jnp.bfloat16)
    projected = jnp.dot(normed, in_weight, preferred_element_type=jnp.float32).astype(jnp.bfloat16)
    taps = short_filter.shape[0]
    earlier = passed_along(projected[tok_rows - (taps - 1) :], "seq", 1)
    extended = jnp.concatenate([earlier, projected], axis=0).astype(jnp.float32)
    mixed = short_filter[0] * extended[taps - 1 :]
    for lag in range(1, taps):
        mixed = mixed + short_filter[lag] * extended[taps - 1 - lag : taps - 1 - lag + tok_rows]
    query = mixed[:, :width].astype(jnp.bfloat16)
    driven = (mixed[:, width : 2 * width] * mixed[:, 2 * width :]).astype(jnp.bfloat16)
    local_cols = inner // devices
    col_start = position * local_cols
    blocked = driven.reshape(tok_rows // inner, inner, width)
    piece = lax.all_to_all(blocked, "seq", split_axis=1, concat_axis=0, tiled=True)
    real_part, imag_part = rows_forward_first(piece, col_start, total)
    spec_real, spec_imag = rows_forward_second(
        (
            lax.all_to_all(
                real_part.astype(jnp.bfloat16), "seq", split_axis=0, concat_axis=1, tiled=True
            ).astype(real_part.dtype),
            lax.all_to_all(
                imag_part.astype(jnp.bfloat16), "seq", split_axis=0, concat_axis=1, tiled=True
            ).astype(imag_part.dtype),
        )
    )
    resident = jnp.transpose(spectra, (0, 2, 3, 1))
    prod_real, prod_imag = apply_filter(spec_real, spec_imag, resident)
    local_rows = outer // devices
    back_real, back_imag = rows_inverse_second(prod_real, prod_imag, position * local_rows, total)
    response_cols = rows_inverse_first(
        (
            lax.all_to_all(
                as_sent(back_real), "seq", split_axis=1, concat_axis=0, tiled=True
            ).astype(back_real.dtype),
            lax.all_to_all(
                as_sent(back_imag), "seq", split_axis=1, concat_axis=0, tiled=True
            ).astype(back_imag.dtype),
        ),
        total,
    )
    response_cols = response_cols + skip_gain[None, None, :] * piece.astype(jnp.float32)
    response = lax.all_to_all(
        response_cols, "seq", split_axis=0, concat_axis=1, tiled=True
    ).reshape(tok_rows, width)
    gated = (query.astype(jnp.float32) * response).astype(jnp.bfloat16)
    hidden_state = (
        tokens.astype(jnp.float32) + jnp.dot(gated, out_weight, preferred_element_type=jnp.float32)
    ).astype(jnp.bfloat16)
    second_norm = rms_scale(hidden_state, mlp_gain).astype(jnp.bfloat16)
    activated = jax.nn.gelu(
        jnp.dot(second_norm, up_weight, preferred_element_type=jnp.float32), approximate=True
    ).astype(jnp.bfloat16)
    return (
        hidden_state.astype(jnp.float32)
        + jnp.dot(activated, down_weight, preferred_element_type=jnp.float32)
    ).astype(jnp.bfloat16)


MESH = pl.DeviceIdType.MESH


def dft_tables(n, outer, inner, groups, share):
    kl = outer // n
    k1 = np.arange(outer)
    ang = 2.0 * np.pi * (np.outer(k1, np.arange(n)) % outer) / outer
    weights = np.stack([np.cos(ang), -np.sin(ang)]).reshape(2, n, kl, n)
    first = np.einsum("rpkn,gh,ij->rgpiknhj", weights, np.eye(groups), np.eye(share))
    first = first.reshape(2 * groups * outer * share, n * groups * share)
    ang = 2.0 * np.pi * (np.outer(np.arange(inner), np.arange(inner)) % inner) / inner
    cos, sin = np.cos(ang), np.sin(ang)
    second = np.block([[cos, -sin], [sin, cos]])
    ang = 2.0 * np.pi * np.outer(k1, np.arange(inner)) / (outer * inner)
    turn = np.stack([np.cos(ang), np.sin(ang)]).reshape(2, n, 1, kl, inner)
    turn = np.broadcast_to(turn, (2, n, share, kl, inner)).reshape(2, n * share * kl, inner)
    low = lambda a: a.astype(ml_dtypes.bfloat16)
    return low(first), low(np.ascontiguousarray(first.T)), low(second), turn.astype(np.float32)


def kernel(
    groups, n, share,
    tokens_hbm, norm_hbm, in_hbm, short_hbm, skip_hbm, mlp_hbm,
    spectra, out_hbm, up_hbm, down_hbm, first_hbm, last_hbm, second_hbm, turn_hbm,
    result,
    tokens, norm_gain, in_weight, short_filter, skip_gain, mlp_gain,
    filt, halo, extended, sent, signal, back, response,
    out_weight, up_weight, down_weight, first, last, second, turn,
    local_sem, filt_send, filt_recv, halo_send, halo_recv,
    sig_send, sig_recv, resp_send, resp_recv,
):
    count = groups * n
    group = lax.axis_index("groups")
    position = lax.axis_index("seq")
    me = position * groups + group
    rows, width = tokens.shape
    taps = short_filter.shape[0]

    def place(index):
        return (lax.rem(index, groups), lax.div(index, groups))

    barrier = pltpu.get_barrier_semaphore()

    def greet(step, carry):
        pl.semaphore_signal(
            barrier, inc=1, device_id=place(lax.rem(me + step, count)), device_id_type=MESH
        )
        return carry

    lax.fori_loop(1, count, greet, 0, unroll=True)

    early = (
        (tokens_hbm, tokens), (norm_hbm, norm_gain), (in_hbm, in_weight),
        (short_hbm, short_filter),
    )
    pairs = early + (
        (first_hbm, first), (second_hbm, second), (turn_hbm, turn), (last_hbm, last),
        (out_hbm, out_weight), (up_hbm, up_weight), (down_hbm, down_weight),
        (skip_hbm, skip_gain), (mlp_hbm, mlp_gain),
    )
    loads = [
        pltpu.make_async_copy(source, target, local_sem.at[i])
        for i, (source, target) in enumerate(pairs)
    ]

    def channels(seq_index):
        return pl.ds((seq_index * groups + group) * share, share)

    own_filter = pltpu.make_async_copy(
        spectra.at[:, channels(position)], filt.at[position], local_sem.at[len(pairs)]
    )

    def filter_copy(target, source):
        return pltpu.make_async_remote_copy(
            src_ref=spectra.at[:, channels(target)], dst_ref=filt.at[source],
            send_sem=filt_send.at[0], recv_sem=filt_recv.at[0],
            device_id=(group, target), device_id_type=MESH,
        )

    def halo_copy(target):
        return pltpu.make_async_remote_copy(
            src_ref=tokens_hbm.at[pl.ds(rows - 16, 16)], dst_ref=halo,
            send_sem=halo_send.at[0], recv_sem=halo_recv.at[0],
            device_id=(group, target), device_id_type=MESH,
        )

    def signal_copy(target, source):
        return pltpu.make_async_remote_copy(
            src_ref=sent.at[target], dst_ref=signal.at[source],
            send_sem=sig_send.at[0], recv_sem=sig_recv.at[0],
            device_id=place(target), device_id_type=MESH,
        )

    def response_copy(target, source):
        return pltpu.make_async_remote_copy(
            src_ref=back.at[target], dst_ref=response.at[source],
            send_sem=resp_send.at[0], recv_sem=resp_recv.at[0],
            device_id=place(target), device_id_type=MESH,
        )

    def all_of(landed, send_sem, recv_sem):
        blocks = landed.at[pl.ds(0, landed.shape[0] - 1)]
        return pltpu.make_async_remote_copy(
            src_ref=blocks, dst_ref=blocks, send_sem=send_sem.at[0], recv_sem=recv_sem.at[0],
            device_id=place(lax.rem(me + groups, count)), device_id_type=MESH,
        )

    def each(total, own, action):
        def body(step, carry):
            action(lax.rem(own + step, total))
            return carry

        lax.fori_loop(1, total, body, 0, unroll=True)

    for load in loads:
        load.start()
    own_filter.start()
    for load in loads[: len(early)]:
        load.wait()
    gain = norm_gain[...].reshape(1, width)
    weight = in_weight[...]

    def project(values):
        normed = rms_scale(values, gain).astype(jnp.bfloat16)
        made = jnp.dot(normed, weight, preferred_element_type=jnp.float32)
        return made.astype(jnp.bfloat16).astype(jnp.float32)

    extended[pl.ds(8, rows), :] = project(tokens[...])

    def drive(start, size):
        mixed = short_filter[0:1, :] * extended[pl.ds(8 + start, size), :]
        for lag in range(1, taps):
            mixed = mixed + short_filter[lag : lag + 1, :] * extended[pl.ds(8 + start - lag, size), :]
        query = mixed[:, :width].astype(jnp.bfloat16).astype(jnp.float32)
        driven = (mixed[:, width : 2 * width] * mixed[:, 2 * width :]).astype(jnp.bfloat16)
        driven = driven.astype(jnp.float32)
        sent[:, :, pl.ds(start, size)] = driven.T.reshape(count, share, size).astype(jnp.bfloat16)
        return query, driven

    head = 128
    query_tail, driven_tail = drive(head, rows - head)

    pl.semaphore_wait(barrier, count - 1)

    @pl.when(position < n - 1)
    def _():
        halo_copy(position + 1).start()

    @pl.when(position == 0)
    def _():
        halo[...] = jnp.zeros_like(halo)

    for step in range(1, (n + 1) // 2):
        filter_copy(lax.rem(position + step, n), position).start()

    @pl.when(position > 0)
    def _():
        halo_copy(position).wait_recv()

    extended[pl.ds(0, 8), :] = project(halo[...])[8:, :]
    query_head, driven_head = drive(0, head)
    query = jnp.concatenate([query_head, query_tail], axis=0)
    driven = jnp.concatenate([driven_head, driven_tail], axis=0)
    each(count, me, lambda other: signal_copy(other, me).start())
    for step in range((n + 1) // 2, n):
        filter_copy(lax.rem(position + step, n), position).start()
    signal[pl.ds(me, 1)] = sent[pl.ds(me, 1)]

    for load in loads[len(early) :]:
        load.wait()
    own_filter.wait()
    all_of(signal, sig_send, sig_recv).wait_recv()

    half = groups * n * share * (filt.shape[3])
    bins = half // groups
    gathered = signal[...].astype(jnp.float32).reshape(count * share, rows).astype(jnp.bfloat16)
    part = jnp.dot(first[...], gathered, preferred_element_type=jnp.float32)
    part_real = part[:half].reshape(groups, bins, rows)
    part_imag = part[half:].reshape(groups, bins, rows)
    turn_cos, turn_sin = turn[0][None], turn[1][None]
    turned = jnp.concatenate(
        [part_real * turn_cos + part_imag * turn_sin, part_imag * turn_cos - part_real * turn_sin],
        axis=-1,
    ).reshape(half, 2 * rows).astype(jnp.bfloat16)
    spec = jnp.dot(turned, second[...], preferred_element_type=jnp.float32)
    spec_real = spec[:, :rows].reshape(groups, bins, rows)
    spec_imag = spec[:, rows:].reshape(groups, bins, rows)
    all_of(filt, filt_send, filt_recv).wait_recv()
    filt_real = filt[:, 0].astype(jnp.float32).reshape(1, bins, rows)
    filt_imag = filt[:, 1].astype(jnp.float32).reshape(1, bins, rows)
    product = jnp.concatenate(
        [
            spec_real * filt_real - spec_imag * filt_imag,
            -(spec_real * filt_imag + spec_imag * filt_real),
        ],
        axis=-1,
    ).reshape(half, 2 * rows).astype(jnp.bfloat16)
    inner_back = jnp.dot(product, second[...], preferred_element_type=jnp.float32)
    back_real = inner_back[:, :rows].reshape(groups, bins, rows)
    back_imag = inner_back[:, rows:].reshape(groups, bins, rows)
    turned_back = jnp.concatenate(
        [
            (back_real * turn_cos + back_imag * turn_sin).reshape(half, rows),
            (back_real * turn_sin - back_imag * turn_cos).reshape(half, rows),
        ],
        axis=0,
    ).astype(jnp.bfloat16)
    total = 2 * n * rows
    conv = jnp.dot(last[...], turned_back, preferred_element_type=jnp.float32) * (1.0 / total)
    back[...] = conv.reshape(count, share, rows).astype(jnp.bfloat16)
    each(count, me, lambda other: response_copy(other, me).start())
    response[pl.ds(me, 1)] = back[pl.ds(me, 1)]
    all_of(response, resp_send, resp_recv).wait_recv()

    answer = response[...].astype(jnp.float32).reshape(width, rows).T
    answer = answer + skip_gain[...].reshape(1, width) * driven
    gated = (query * answer).astype(jnp.bfloat16)
    hidden = (
        tokens[...].astype(jnp.float32)
        + jnp.dot(gated, out_weight[...], preferred_element_type=jnp.float32)
    ).astype(jnp.bfloat16)
    second_norm = rms_scale(hidden, mlp_gain[...].reshape(1, width)).astype(jnp.bfloat16)
    activated = jax.nn.gelu(
        jnp.dot(second_norm, up_weight[...], preferred_element_type=jnp.float32), approximate=True
    ).astype(jnp.bfloat16)
    result[...] = (
        hidden.astype(jnp.float32)
        + jnp.dot(activated, down_weight[...], preferred_element_type=jnp.float32)
    ).astype(jnp.bfloat16)

    @pl.when(position < n - 1)
    def _():
        halo_copy(position + 1).wait_send()

    all_of(filt, filt_send, filt_recv).wait_send()
    all_of(signal, sig_send, sig_recv).wait_send()
    all_of(response, resp_send, resp_recv).wait_send()


def fused(
    tokens, norm_gain, in_weight, short_filter, spectra, skip_gain,
    out_weight, mlp_gain, up_weight, down_weight,
):
    rows, width = tokens.shape
    groups, n = lax.axis_size("groups"), lax.axis_size("seq")
    count = groups * n
    share = width // count
    local_outer = spectra.shape[2]
    first, last, second, turn = dft_tables(n, n * local_outer, rows, groups, share)
    low = jnp.bfloat16
    vmem = pl.BlockSpec(memory_space=pltpu.VMEM)
    far = pl.BlockSpec(memory_space=pltpu.HBM)
    dma = pltpu.SemaphoreType.DMA
    small = [tokens, norm_gain, in_weight, short_filter, skip_gain, mlp_gain]
    held = [out_weight, up_weight, down_weight, first, last, second, turn]
    return pl.pallas_call(
        functools.partial(kernel, groups, n, share),
        out_shape=pltpu.VMEM((rows, width), low),
        in_specs=[far] * 14,
        out_specs=vmem,
        scratch_shapes=[pltpu.VMEM(a.shape, a.dtype) for a in small]
        + [
            pltpu.VMEM((n, 2, share, local_outer, rows), low),
            pltpu.VMEM((16, width), low),
            pltpu.VMEM((rows + 8, 3 * width), jnp.float32),
            pltpu.VMEM((count, share, rows), low),
            pltpu.VMEM((count, share, rows), low),
            pltpu.VMEM((count, share, rows), low),
            pltpu.VMEM((count, share, rows), low),
        ]
        + [pltpu.VMEM(a.shape, a.dtype) for a in held]
        + [
            dma((16,)), dma((1,)), dma((1,)), dma((1,)), dma((1,)),
            dma((1,)), dma((1,)), dma((1,)), dma((1,)),
        ],
        compiler_params=pltpu.CompilerParams(
            collective_id=0, has_side_effects=True, vmem_limit_bytes=56 * 1024 * 1024
        ),
    )(
        tokens, norm_gain, in_weight, short_filter, skip_gain, mlp_gain,
        spectra, out_weight, up_weight, down_weight, first, last, second, turn,
    )


def solution(mesh):
    in_specs = (
        P(("groups", "seq"), None),
        P(),
        P(),
        P(),
        P(None, None, "seq", None),
        P(),
        P(),
        P(),
        P(),
        P(),
    )
    out_specs = P(("groups", "seq"), None)

    def layer(*args):
        rows, width = args[0].shape
        spectra = args[4]
        fits = (
            width % (8 * mesh.size) == 0
            and rows == spectra.shape[3]
            and spectra.shape[2] == 2
            and rows % 128 == 0
            and rows > 128
        )
        return (fused if fits else local)(*args)

    return jax.shard_map(layer, mesh=mesh, in_specs=in_specs, out_specs=out_specs, check_vma=False)
```
